128 devices in a mesh: deg: 16 (over y, x_hi, core), row: 8 (over z, x_lo).
Axes of the slice: x: 4 (x_hi: 2, x_lo: 2; x = x_hi * 2 + x_lo), y: 4, z: 4, core: 2. Of those that a mesh axis runs over, the one named last changes fastest.
Arguments:
- left: float32 [16384, 4096], P('deg', 'row'), may hold values from 0 to 7340032, as said below
- right: float32 [16384, 1024], P('deg', 'row'), may hold values from 0 to 7340032, as said below
Outputs:
- product_scaled: float32 [32768, 1024], P('deg', 'row')
The draws below stay inside these ranges and needn't reach their ends.
Inputs may be any that keep to these rules, and one draw needn't show every extreme that they name: `left`: every entry is an integer residue modulo the prime 7340033. `right`: every entry is an integer residue modulo the prime 7340033.
All inputs are finite; a program needn't handle non-finite values.
Results may differ from the reference program's by a relative error of at most 0.0003.
Values sent between devices are 32-bit elements; how exact they have to be, the bound alone decides.
No kernel may reach another device: no remote copies, remote signals or barrier semaphores. Data moves between devices by JAX's collectives and lax.ppermute only.
A program may use at most 256 MiB of HBM per device.

```python
import jax
import jax.numpy as jnp
import numpy as np
from jax import lax

DEG = 16384
K = 64
COLS = 16
ROWS_DEV = 8
ROWS = 64
N_ROW = 8


def residues(key, rows, columns):
    values = jax.random.randint(key, (rows, columns), 0, 7340033).astype(jnp.float32)
    return values


def draw_left(key, part):
    key = jax.random.fold_in(key, 1)
    return residues(key, DEG, ROWS * K)


def draw_right(key, part):
    key = jax.random.fold_in(key, 2)
    return residues(key, DEG, K * COLS)


def setup_inputs(seed: int = 0) -> dict:
    keys = jax.random.split(jax.random.key(seed), 3)
    left = draw_left(jax.random.fold_in(keys[2], 71), 0)
    right = draw_right(jax.random.fold_in(keys[2], 71), 0)
    return {"left": left, "right": right}


modulus = 7340033
inv_modulus = 1.0 / 7340033.0
generator = 3


def power_list(unit_root, entries):
    values = np.ones(entries, dtype=np.int64)
    current = 1
    for position in range(entries):
        values[position] = current
        current = current * unit_root % modulus
    return values


def root_of(period, inverse):
    element = pow(generator, (modulus - 1) // period, modulus)
    return pow(element, modulus - 2, modulus) if inverse else element


def add_mod(first, second):
    summed = first + second
    return jnp.where(summed >= modulus, summed - modulus, summed)


def sub_mod(first, second):
    differ = first - second
    return jnp.where(differ < 0, differ + modulus, differ)


def mul_mod(first, second):
    quotient = jnp.floor(first * second * inv_modulus)
    residual = first.astype(jnp.int32) * second.astype(jnp.int32) - quotient.astype(jnp.int32) * modulus
    return jnp.remainder(residual, modulus).astype(first.dtype)


def transform(values, dimension, unit_root):
    length = values.shape[dimension]
    powers = power_list(unit_root, length)
    leading = values.shape[:dimension]
    trailing = values.shape[dimension + 1:]
    current = values.reshape(leading + (1, length) + trailing)
    stride = 1
    while stride < length:
        half_size = current.shape[dimension + 1] // 2
        even_part = lax.slice_in_dim(current, 0, half_size, axis=dimension + 1)
        odd_part = lax.slice_in_dim(current, half_size, 2 * half_size, axis=dimension + 1)
        factor = powers[(length // (2 * stride)) * np.arange(stride)]
        factor = jnp.asarray(factor, dtype=jnp.float32).reshape((1,) * len(leading) + (stride, 1) + (1,) * len(trailing))
        twisted = mul_mod(odd_part, factor)
        current = jnp.concatenate([add_mod(even_part, twisted), sub_mod(even_part, twisted)], axis=dimension)
        stride = stride * 2
    return current.reshape(leading + (length,) + trailing)


def digits_of(values):
    high_digit = jnp.floor(values * (1.0 / 65536.0))
    remaining = values - high_digit * 65536.0
    middle = jnp.floor(remaining * (1.0 / 256.0))
    low_digit = remaining - middle * 256.0
    return (low_digit, middle, high_digit)


def fold_sums(digit_sums):
    combined = None
    for shift in range(5):
        weight = jnp.asarray(float(pow(2, 8 * shift, modulus)), dtype=jnp.float32)
        scaled_term = mul_mod(digit_sums[shift], weight)
        combined = scaled_term if combined is None else add_mod(combined, scaled_term)
    return combined


def reference(left, right):
    length = 2 * DEG
    forward_root = root_of(length, False)
    backward_root = root_of(length, True)
    scale_back = jnp.asarray(float(pow(length, modulus - 2, modulus)), dtype=jnp.float32)
    padded_right = jnp.concatenate([right, jnp.zeros_like(right)], axis=0)
    right_eval = transform(padded_right, 0, forward_root).reshape(length, K, COLS)
    right_digits = digits_of(right_eval)

    def one_group(group_index):
        left_block = lax.dynamic_slice_in_dim(left, group_index * ROWS_DEV * K, ROWS_DEV * K, 1)
        left_block = jnp.concatenate([left_block, jnp.zeros_like(left_block)], axis=0)
        left_eval = transform(left_block, 0, forward_root).reshape(length, ROWS_DEV, K)
        left_digits = digits_of(left_eval)
        digit_sums = [jnp.zeros((length, ROWS_DEV, COLS), jnp.float32) for shift in range(5)]
        for first_digit in range(3):
            for second_digit in range(3):
                digit_sums[first_digit + second_digit] = digit_sums[first_digit + second_digit] + jnp.einsum(
                    "prk,pkc->prc", left_digits[first_digit].astype(jnp.float32),
                    right_digits[second_digit].astype(jnp.float32), precision=lax.Precision.HIGHEST)
        product = fold_sums(digit_sums)
        coefficients = transform(product, 0, backward_root)
        coefficients = mul_mod(coefficients, scale_back)
        return coefficients.reshape(length, ROWS_DEV * COLS)

    grouped = lax.map(one_group, jnp.arange(N_ROW, dtype=jnp.int32))
    whole = jnp.moveaxis(grouped, 0, 1).reshape(length, ROWS * COLS)
    return whole / 7340033.0
```

```python
import jax
import jax.numpy as jnp
import numpy as np
from jax import lax
from jax.experimental import pallas as pl
from jax.experimental.pallas import tpu as pltpu
from jax.sharding import PartitionSpec as P

K = 64
COLS = 16
modulus = 7340033
generator = 3

BLOCK = 1024
POINTS = 2048
N_DEG = 16
N_ROW = 8
N_DEV = N_DEG * N_ROW
PER = POINTS // N_DEV
FACTORS = (64, 32)
AXES = ("deg", "row")
VMEM_LIMIT = 60 * 1024 * 1024

ROUND = 1.5 * 2.0**23
ROUND_8 = ROUND * 2.0**8
ROUND_16 = ROUND * 2.0**16
HIGH = 7.0 * 2.0**20


def root_powers(order):
    root = pow(generator, (modulus - 1) // order, modulus)
    values = np.ones(order, dtype=np.int64)
    for position in range(1, order):
        values[position] = values[position - 1] * root % modulus
    return values


def digit_matrix(matrix):
    columns = []
    for a in range(3):
        value = matrix * pow(2, 8 * a, modulus) % modulus
        value = np.where(value > modulus // 2, value - modulus, value)
        low = ((value + 128) & 255) - 128
        value = (value - low) >> 8
        middle = ((value + 128) & 255) - 128
        high = (value - middle) >> 8
        rows = np.concatenate([low, middle, high], axis=-2)
        columns.append(rows * 2.0 ** (-8 * a))
    return np.concatenate(columns, axis=-1).astype(np.float32)


def forward_tables():
    powers = root_powers(POINTS)
    k1, m1, m0 = np.arange(64), np.arange(32), np.arange(32)
    first = powers[(32 * m1[None, None, :] + m0[:, None, None]) * k1[None, :, None] % POINTS]
    k0 = np.arange(32)
    second = powers[64 * k0[:, None] * m0[None, :] % POINTS]
    return digit_matrix(first), digit_matrix(second)


def backward_tables():
    powers = root_powers(POINTS)
    k1, k0, m0, m1 = np.arange(64), np.arange(32), np.arange(32), np.arange(32)
    exponent = m0[None, :, None] * (64 * k0[None, None, :] + k1[:, None, None])
    first = powers[-exponent % POINTS] * pow(POINTS, modulus - 2, modulus) % modulus
    second = powers[-32 * m1[:, None] * k1[None, :] % POINTS]
    return digit_matrix(first), digit_matrix(second)


def split(value):
    high = (value + ROUND_16) - ROUND_16
    rest = value - high
    middle = (rest + ROUND_8) - ROUND_8
    return rest - middle, middle, high


def digit_rows(value):
    return jnp.concatenate([digit.astype(jnp.bfloat16) for digit in split(value)], axis=0)


def fold(sums):
    s0, s1, s2 = sums
    quotient = s2 * (65536.0 / modulus) + s1 * (256.0 / modulus)
    quotient = (quotient + ROUND) - ROUND
    return ((s2 * 65536.0 - quotient * HIGH) + s1 * 256.0) + (s0 - quotient)


def times_256(value):
    quotient = (value * (256.0 / modulus) + ROUND) - ROUND
    return (value * 256.0 - quotient * HIGH) - quotient


def matmul(first, second):
    return jnp.dot(first, second, preferred_element_type=jnp.float32)


def thirds(value):
    rows = value.shape[0] // 3
    return value[:rows], value[rows : 2 * rows], value[2 * rows :]


def forward_kernel(first_ref, second_ref, *refs):
    tiles = len(refs) // 2
    x_refs, out_ref, middle_refs = refs[:tiles], refs[tiles], refs[tiles + 1 :]

    def first_step(m0, carry):
        value = jnp.concatenate([ref[pl.ds(m0, 32, stride=32), :] for ref in x_refs], axis=1)
        value = fold(thirds(matmul(first_ref[m0], digit_rows(value))))
        for tile, ref in enumerate(middle_refs):
            ref[pl.ds(m0, 64, stride=32), :] = value[:, 128 * tile : 128 * tile + 128]
        return carry

    lax.fori_loop(0, 32, first_step, 0, unroll=2)
    second = second_ref[...]

    def second_step(k1, carry):
        rows = pl.ds(pl.multiple_of(k1 * 32, 32), 32)
        value = jnp.concatenate([ref[rows, :] for ref in middle_refs], axis=1)
        out_ref[rows, :] = fold(thirds(matmul(second, digit_rows(value))))
        return carry

    lax.fori_loop(0, 64, second_step, 0, unroll=2)


def forward(block, lanes):
    first, second = (jnp.asarray(table, dtype=jnp.bfloat16) for table in forward_tables())
    columns = block.shape[1]
    tiles = lanes // 128
    return pl.pallas_call(
        forward_kernel,
        grid=(columns // lanes,),
        in_specs=[
            pl.BlockSpec(first.shape, lambda step: (0, 0, 0)),
            pl.BlockSpec(second.shape, lambda step: (0, 0)),
        ]
        + [
            pl.BlockSpec((BLOCK, 128), lambda step, tile=tile: (0, step * tiles + tile))
            for tile in range(tiles)
        ],
        out_specs=pl.BlockSpec((POINTS, lanes), lambda step: (0, step)),
        out_shape=jax.ShapeDtypeStruct((POINTS, columns), jnp.float32),
        scratch_shapes=[pltpu.VMEM((POINTS, 128), jnp.float32)] * tiles,
        compiler_params=pltpu.CompilerParams(vmem_limit_bytes=VMEM_LIMIT),
        name="forward",
    )(first, second, *[block] * tiles)


def backward_kernel(first_ref, second_ref, x_ref, out_ref, *middle_refs):
    def first_step(k1, carry):
        halves = []
        for e in range(2):
            start = k1 * 64 + e * PER
            halves.append(
                jnp.concatenate(
                    [
                        x_ref[pl.ds(pl.multiple_of(start + 32 * part, PER), PER), :]
                        for part in range(2)
                    ],
                    axis=0,
                )
            )
        data = digit_rows(jnp.concatenate(halves, axis=1))
        value = fold(thirds(matmul(first_ref[k1], data)))
        for e, ref in enumerate(middle_refs):
            ref[pl.ds(k1, 32, stride=64), :] = value[:, e * 128 : e * 128 + 128]
        return carry

    lax.fori_loop(0, 64, first_step, 0, unroll=2)
    second = second_ref[...]

    def second_step(m0, carry):
        rows = pl.ds(pl.multiple_of(m0 * 64, 64), 64)
        value = jnp.concatenate([ref[rows, :] for ref in middle_refs], axis=1)
        value = fold(thirds(matmul(second, digit_rows(value))))
        value = jnp.where(value < 0.0, value + float(modulus), value) / float(modulus)
        for e in range(2):
            out_ref[pl.ds(e * BLOCK + m0, 32, stride=32), :] = value[:, e * 128 : (e + 1) * 128]
        return carry

    lax.fori_loop(0, 32, second_step, 0, unroll=2)


def backward(values):
    first, second = (jnp.asarray(table, dtype=jnp.bfloat16) for table in backward_tables())
    return pl.pallas_call(
        backward_kernel,
        out_shape=jax.ShapeDtypeStruct((2 * BLOCK, 128), jnp.float32),
        scratch_shapes=[pltpu.VMEM((POINTS, 128), jnp.float32)] * 2,
        compiler_params=pltpu.CompilerParams(vmem_limit_bytes=VMEM_LIMIT),
        name="backward",
    )(first, second, values)


def swap_groups(tiles):
    tiles = list(tiles)
    group = lax.broadcasted_iota(jnp.int32, tiles[0].shape, 1) // 16
    for bit in (1, 2, 4):
        keep = (group & bit) == 0
        for low in range(8):
            if low & bit:
                continue
            first, second = tiles[low], tiles[low + bit]
            tiles[low] = jnp.where(keep, first, pltpu.roll(second, 16 * bit, 1))
            tiles[low + bit] = jnp.where(keep, pltpu.roll(first, 128 - 16 * bit, 1), second)
    return tiles


def product_kernel(sign_ref, *refs):
    left_refs, right_ref, out_ref = refs[:4], refs[4], refs[5]
    right_scrs, weight_scr, left_scr, sum_scr, value_scr = refs[6:8], *refs[8:]
    lane = lax.broadcasted_iota(jnp.int32, (8, 128), 1)
    low_half = lane < 64
    sign = sign_ref[0]

    def point(k, carry):
        for half in range(2):
            tiles = [
                right_ref[pl.ds((half * 8 + d) * 8 * PER + k, 8, stride=PER), :] for d in range(8)
            ]
            for i8, tile in enumerate(swap_groups(tiles)):
                right_scrs[half][pl.ds(i8, 8, stride=8), :] = tile
        value = jnp.concatenate([scr[...] for scr in right_scrs], axis=1)
        for a in range(3):
            if a:
                value = times_256(value)
            for b, digit in enumerate(split(value)):
                digit = (digit * 2.0 ** (-8 * (a + b))).astype(jnp.bfloat16)
                weight_scr[a * 64 : a * 64 + 64, b * 256 : b * 256 + 256] = digit
                if a == 2:
                    weight_scr[192:256, b * 256 : b * 256 + 256] = digit
        for pair in range(4):
            rows = [[], []]
            for d in range(N_DEG):
                tile = left_refs[pair][pl.ds(d * 8 * PER + k, 8, stride=PER), :]
                d0, d1, d2 = split(tile)
                d0_other, d1_other = pltpu.roll(d0, 64, 1), pltpu.roll(d1, 64, 1)
                rows[0].append(
                    (jnp.where(low_half, d0, d1_other), jnp.where(low_half, d2, 0.0))
                )
                rows[1].append(
                    (jnp.where(low_half, d0_other, d1), jnp.where(low_half, 0.0, d2))
                )
            for odd in range(2):
                start = (2 * pair + odd) * 128
                for part in range(2):
                    left_scr[start : start + 128, part * 128 : part * 128 + 128] = jnp.concatenate(
                        [row[part] for row in rows[odd]], axis=0
                    ).astype(jnp.bfloat16)
        sum_scr[...] = matmul(left_scr[...], weight_scr[...])

        def one_row(r8, carry):
            base = pl.multiple_of(r8 * 128, 128)
            totals = []
            for b in range(3):
                total = None
                for group in ((0, 1, 2), (3, 4, 5), (6, 7)):
                    parts = [0.0] * 4
                    for shift in group:
                        tiles = [
                            [
                                sum_scr[
                                    pl.ds(base + (8 * high + shift) * 8, 8),
                                    b * 256 + 128 * t : b * 256 + 128 * t + 128,
                                ]
                                for t in range(2)
                            ]
                            for high in range(2)
                        ]
                        tiles = [tiles[0][0], tiles[0][1] + tiles[1][0], tiles[1][1]]
                        if shift:
                            tiles = [pltpu.roll(tile, 16 * shift, 1) for tile in tiles]
                            keep = lane >= 16 * shift
                            tiles = [
                                jnp.where(keep, tiles[0], 0.0),
                                jnp.where(keep, tiles[1], tiles[0]),
                                jnp.where(keep, tiles[2], tiles[1]),
                                jnp.where(keep, 0.0, tiles[2]),
                            ]
                        parts = [
                            part + tile for part, tile in zip(parts, tiles + [0.0] * (4 - len(tiles)))
                        ]
                    parts = [part.astype(jnp.int32) for part in parts]
                    total = parts if total is None else [x + y for x, y in zip(total, parts)]
                totals.append(total)
            before = jnp.zeros((8, 128), jnp.float32)
            for t in range(4):
                s0, s1, s2 = (total[t] for total in totals)
                quotient = (
                    s2.astype(jnp.float32) * (65536.0 / modulus)
                    + s1.astype(jnp.float32) * (256.0 / modulus)
                    + s0.astype(jnp.float32) * (1.0 / modulus)
                )
                quotient = ((quotient + ROUND) - ROUND).astype(jnp.int32)
                rest = (s2 << 16) + (s1 << 8) + s0 - quotient - ((quotient * 7) << 20)
                value = rest.astype(jnp.float32)
                shifted = pltpu.roll(value, 16, 1)
                value_scr[pl.ds(pl.multiple_of(r8 * 8, 8), 8), t * 128 : t * 128 + 128] = (
                    value + sign * jnp.where(lane < 16, before, shifted)
                )
                before = shifted
            return carry

        lax.fori_loop(0, 8, one_row, 0)
        for t in range(4):
            tiles = [value_scr[r8 * 8 : r8 * 8 + 8, t * 128 : t * 128 + 128] for r8 in range(8)]
            for g, tile in enumerate(swap_groups(tiles)):
                e = 8 * t + g
                start = (e // 2) * 8 * 2 * PER + (e % 2) * PER
                out_ref[pl.ds(start + k, 8, stride=2 * PER), :] = tile
        return carry

    lax.fori_loop(0, PER, point, 0)


def product(sign, left, right):
    return pl.pallas_call(
        product_kernel,
        grid=(1,),
        in_specs=[pl.BlockSpec(memory_space=pltpu.SMEM)]
        + [
            pl.BlockSpec((POINTS, 128), lambda step, tile=tile: (0, tile)) for tile in range(4)
        ]
        + [pl.BlockSpec((POINTS, 128), lambda step: (0, 0))],
        out_specs=pl.BlockSpec((2 * POINTS, 128), lambda step: (0, 0)),
        out_shape=jax.ShapeDtypeStruct((2 * POINTS, 128), jnp.float32),
        scratch_shapes=[
            pltpu.VMEM((64, 128), jnp.float32),
            pltpu.VMEM((64, 128), jnp.float32),
            pltpu.VMEM((256, 768), jnp.bfloat16),
            pltpu.VMEM((1024, 256), jnp.bfloat16),
            pltpu.VMEM((1024, 768), jnp.float32),
            pltpu.VMEM((64, 512), jnp.float32),
        ],
        compiler_params=pltpu.CompilerParams(vmem_limit_bytes=VMEM_LIMIT),
        name="product",
    )(sign, *[left] * 4, right)


def exchange(values, rows):
    parts = values.reshape(N_DEV, rows, values.shape[1])
    moved = lax.all_to_all(parts, AXES, split_axis=0, concat_axis=0, tiled=True)
    return moved.reshape(values.shape)


def on_device(left, right):
    mine = lax.axis_index("deg") * N_ROW + lax.axis_index("row")
    sign = (1 - 2 * ((mine // 2) % 2)).astype(jnp.float32).reshape(1)
    right_points = exchange(forward(right, 128), PER)
    left_points = exchange(forward(left, 256), PER)
    values = product(sign, left_points, right_points)
    return backward(exchange(values, 2 * PER))


def solution(mesh):
    return jax.shard_map(
        on_device,
        mesh=mesh,
        in_specs=(P("deg", "row"), P("deg", "row")),
        out_specs=P("deg", "row"),
        check_vma=False,
    )
```

```python
import functools

import jax
import jax.numpy as jnp
import numpy as np
from jax import lax
from jax.experimental import pallas as pl
from jax.experimental.pallas import tpu as pltpu
from jax.sharding import PartitionSpec as P

K = 64
COLS = 16
modulus = 7340033
generator = 3

BLOCK = 1024
POINTS = 2048
N_DEG = 16
N_ROW = 8
N_DEV = N_DEG * N_ROW
PER = POINTS // N_DEV
FACTORS = (64, 32)
AXES = ("deg", "row")
CHUNKS = 2
CHUNK_ROWS = 4
STEP = 2
PITCH = 40
PITCH_BACK = 72
UNROLL = 16
VMEM_LIMIT = 60 * 1024 * 1024

ROUND = 1.5 * 2.0**23
ROUND_8 = ROUND * 2.0**8
ROUND_16 = ROUND * 2.0**16
HIGH = 7.0 * 2.0**20


def root_powers(order):
    root = pow(generator, (modulus - 1) // order, modulus)
    values = np.ones(order, dtype=np.int64)
    for position in range(1, order):
        values[position] = values[position - 1] * root % modulus
    return values


def digit_matrix(matrix):
    columns = []
    for a in range(3):
        value = matrix * pow(2, 8 * a, modulus) % modulus
        value = np.where(value > modulus // 2, value - modulus, value)
        low = ((value + 128) & 255) - 128
        value = (value - low) >> 8
        middle = ((value + 128) & 255) - 128
        high = (value - middle) >> 8
        rows = np.concatenate([low, middle, high], axis=-2)
        columns.append(rows * 2.0 ** (-8 * a))
    return np.concatenate(columns, axis=-1).astype(np.float32)


def forward_tables():
    powers = root_powers(POINTS)
    k1, m1, m0 = np.arange(64), np.arange(32), np.arange(32)
    first = powers[(32 * m1[None, None, :] + m0[:, None, None]) * k1[None, :, None] % POINTS]
    k0 = np.arange(32)
    second = powers[64 * k0[:, None] * m0[None, :] % POINTS]
    return digit_matrix(first), digit_matrix(second)


def backward_tables():
    powers = root_powers(POINTS)
    k1, k0, m0, m1 = np.arange(64), np.arange(32), np.arange(32), np.arange(32)
    exponent = m0[None, :, None] * (64 * k0[None, None, :] + k1[:, None, None])
    first = powers[-exponent % POINTS] * pow(POINTS, modulus - 2, modulus) % modulus
    second = powers[-32 * m1[:, None] * k1[None, :] % POINTS]
    return digit_matrix(first), digit_matrix(second)


def split(value):
    high = (value + ROUND_16) - ROUND_16
    rest = value - high
    middle = (rest + ROUND_8) - ROUND_8
    return rest - middle, middle, high


def digit_rows(value):
    return jnp.concatenate([digit.astype(jnp.bfloat16) for digit in split(value)], axis=0)


def fold(sums):
    s0, s1, s2 = sums
    quotient = s2 * (65536.0 / modulus) + s1 * (256.0 / modulus)
    quotient = (quotient + ROUND) - ROUND
    return ((s2 * 65536.0 - quotient * HIGH) + s1 * 256.0) + (s0 - quotient)


def times_256(value):
    quotient = (value * (256.0 / modulus) + ROUND) - ROUND
    return (value * 256.0 - quotient * HIGH) - quotient


def matmul(first, second):
    return jnp.dot(first, second, preferred_element_type=jnp.float32)


def thirds(value):
    rows = value.shape[0] // 3
    return value[:rows], value[rows : 2 * rows], value[2 * rows :]


def forward_kernel(tiles, first_ref, second_ref, *refs):
    x_refs, out_ref, middle_refs = refs[:tiles], refs[tiles], refs[tiles + 1 :]

    def first_step(m0, carry):
        value = jnp.concatenate([ref[pl.ds(m0, 32, stride=32), :] for ref in x_refs], axis=1)
        value = fold(thirds(matmul(first_ref[m0], digit_rows(value))))
        for tile, ref in enumerate(middle_refs):
            ref[pl.ds(m0, 64, stride=PITCH), :] = value[:, 128 * tile : 128 * tile + 128]
        return carry

    lax.fori_loop(0, 32, first_step, 0, unroll=UNROLL)
    second = second_ref[...]

    def second_step(k1, carry):
        rows = pl.ds(pl.multiple_of(k1 * PITCH, 8), 32)
        value = jnp.concatenate([ref[rows, :] for ref in middle_refs], axis=1)
        rows = pl.ds(pl.multiple_of(k1 * 32, 32), 32)
        out_ref[rows, :] = fold(thirds(matmul(second, digit_rows(value))))
        return carry

    lax.fori_loop(0, 64, second_step, 0, unroll=UNROLL)


def forward(*columns):
    first, second = (jnp.asarray(table, dtype=jnp.bfloat16) for table in forward_tables())
    tiles = len(columns)
    return pl.pallas_call(
        functools.partial(forward_kernel, tiles),
        grid=(1,),
        in_specs=[
            pl.BlockSpec(first.shape, lambda step: (0, 0, 0)),
            pl.BlockSpec(second.shape, lambda step: (0, 0)),
        ]
        + [
            pl.BlockSpec((BLOCK, 128), lambda step, tile=tile: (0, tile)) for _, tile in columns
        ],
        out_specs=pl.BlockSpec((POINTS, tiles * 128), lambda step: (0, 0)),
        out_shape=jax.ShapeDtypeStruct((POINTS, tiles * 128), jnp.float32),
        scratch_shapes=[pltpu.VMEM((64 * PITCH, 128), jnp.float32)] * tiles,
        compiler_params=pltpu.CompilerParams(vmem_limit_bytes=VMEM_LIMIT),
        cost_estimate=pl.CostEstimate(
            flops=tiles * 3 * 10**9, bytes_accessed=tiles * 3 * 2**19, transcendentals=0
        ),
        name="forward",
    )(first, second, *[array for array, _ in columns])


def backward_kernel(first_ref, second_ref, *refs):
    x_refs, out_ref, middle_refs = refs[:CHUNKS], refs[CHUNKS], refs[CHUNKS + 1 :]
    low_half = lax.broadcasted_iota(jnp.int32, (32, 128), 1) < 64

    def first_step(k1, carry):
        rows = pl.ds(pl.multiple_of(k1 * 32, 32), 32)
        data = digit_rows(jnp.concatenate([ref[rows, :] for ref in x_refs], axis=1))
        value = fold(thirds(matmul(first_ref[k1], data)))
        for chunk, ref in enumerate(middle_refs):
            ref[pl.ds(k1, 32, stride=PITCH_BACK), :] = value[:, chunk * 128 : chunk * 128 + 128]
        return carry

    lax.fori_loop(0, 64, first_step, 0, unroll=UNROLL)
    second = second_ref[...]

    def second_step(m0, carry):
        rows = pl.ds(pl.multiple_of(m0 * PITCH_BACK, 8), 64)
        value = jnp.concatenate([ref[rows, :] for ref in middle_refs], axis=1)
        value = fold(thirds(matmul(second, digit_rows(value))))
        value = jnp.where(value < 0.0, value + float(modulus), value) / float(modulus)
        low, high = value[:, :128], value[:, 128:]
        out_ref[pl.ds(m0, 32, stride=32), :] = jnp.where(low_half, low, pltpu.roll(high, 64, 1))
        out_ref[pl.ds(BLOCK + m0, 32, stride=32), :] = jnp.where(
            low_half, pltpu.roll(low, 64, 1), high
        )
        return carry

    lax.fori_loop(0, 32, second_step, 0, unroll=UNROLL)


def backward(chunks):
    first, second = (jnp.asarray(table, dtype=jnp.bfloat16) for table in backward_tables())
    return pl.pallas_call(
        backward_kernel,
        out_shape=jax.ShapeDtypeStruct((2 * BLOCK, 128), jnp.float32),
        scratch_shapes=[pltpu.VMEM((32 * PITCH_BACK, 128), jnp.float32)] * CHUNKS,
        compiler_params=pltpu.CompilerParams(vmem_limit_bytes=VMEM_LIMIT),
        cost_estimate=pl.CostEstimate(
            flops=8 * 10**9, bytes_accessed=3 * 2**20, transcendentals=0
        ),
        name="backward",
    )(first, second, *chunks)


def exchange_bit(tiles, index_bit, group_bit):
    tiles = list(tiles)
    lane = lax.broadcasted_iota(jnp.int32, tiles[0].shape, 1)
    keep = (lane & (16 * group_bit)) == 0
    for low in range(len(tiles)):
        if low & index_bit:
            continue
        first, second = tiles[low], tiles[low + index_bit]
        tiles[low] = jnp.where(keep, first, pltpu.roll(second, 16 * group_bit, 1))
        tiles[low + index_bit] = jnp.where(
            keep, pltpu.roll(first, 128 - 16 * group_bit, 1), second
        )
    return tiles


def weights_kernel(right_ref, out_ref, *scratch):
    step = pl.program_id(0)
    for point in range(STEP):
        scrs = scratch[2 * point : 2 * point + 2]
        for half in range(2):
            tiles = [
                right_ref[pl.ds((half * 8 + d) * 8 * PER + STEP * step + point, 8, stride=PER), :]
                for d in range(8)
            ]
            for bit in (1, 2, 4):
                tiles = exchange_bit(tiles, bit, bit)
            for i8, tile in enumerate(tiles):
                scrs[half][pl.ds(i8, 8, stride=8), :] = tile
        value = jnp.concatenate([scr[...] for scr in scrs], axis=1)
        for a in range(3):
            if a:
                value = times_256(value)
            for b, digit in enumerate(split(value)):
                digit = (digit * 2.0 ** (-8 * (a + b))).astype(jnp.bfloat16)
                out_ref[point, a * 64 : a * 64 + 64, b * 256 : b * 256 + 256] = digit
                if a == 2:
                    out_ref[point, 192:256, b * 256 : b * 256 + 256] = digit


def weights(points, tile):
    return pl.pallas_call(
        weights_kernel,
        grid=(PER // STEP,),
        in_specs=[pl.BlockSpec((POINTS, 128), lambda step: (0, tile))],
        out_specs=pl.BlockSpec((STEP, 256, 768), lambda step: (step, 0, 0)),
        out_shape=jax.ShapeDtypeStruct((PER, 256, 768), jnp.bfloat16),
        scratch_shapes=[pltpu.VMEM((64, 128), jnp.float32)] * (2 * STEP),
        compiler_params=pltpu.CompilerParams(vmem_limit_bytes=VMEM_LIMIT),
        cost_estimate=pl.CostEstimate(
            flops=3 * 10**9, bytes_accessed=7 * 2**20, transcendentals=0
        ),
        name="weights",
    )(points)


def product_kernel(sign_ref, *refs):
    left_refs, weight_ref, out_ref = refs[:2], refs[2], refs[3]
    left_scrs, sum_scrs = refs[4 : 4 + STEP], refs[4 + STEP :]
    step = pl.program_id(0)
    lane = lax.broadcasted_iota(jnp.int32, (8, 128), 1)
    low_half = lane < 64
    sign = sign_ref[0]

    def prepare(point):
        for pair in range(CHUNK_ROWS // 2):
            rows = [[], []]
            for d in range(N_DEG):
                tile = left_refs[pair][
                    pl.ds(d * 8 * PER + STEP * step + point, 8, stride=PER), :
                ]
                d0, d1, d2 = split(tile)
                d0_other, d1_other = pltpu.roll(d0, 64, 1), pltpu.roll(d1, 64, 1)
                rows[0].append(
                    (jnp.where(low_half, d0, d1_other), jnp.where(low_half, d2, 0.0))
                )
                rows[1].append(
                    (jnp.where(low_half, d0_other, d1), jnp.where(low_half, 0.0, d2))
                )
            for odd in range(2):
                start = (2 * pair + odd) * 128
                for part in range(2):
                    left_scrs[point][start : start + 128, part * 128 : part * 128 + 128] = (
                        jnp.concatenate([row[part] for row in rows[odd]], axis=0).astype(
                            jnp.bfloat16
                        )
                    )

    def multiply(point):
        sum_scrs[point][...] = matmul(left_scrs[point][...], weight_ref[point])

    def shifted_sums(sum_scr, r4, b):
        total = None
        for group in ((0, 1, 2), (3, 4, 5), (6, 7)):
            parts = None
            for shift in group:
                tiles = [
                    [
                        sum_scr[
                            pl.ds(r4 * 128 + (8 * high + shift) * 8, 8),
                            b * 256 + 128 * t : b * 256 + 128 * t + 128,
                        ]
                        for t in range(2)
                    ]
                    for high in range(2)
                ]
                tiles = [tiles[0][0], tiles[0][1] + tiles[1][0], tiles[1][1]]
                if shift:
                    tiles = [pltpu.roll(tile, 16 * shift, 1) for tile in tiles]
                    keep = lane >= 16 * shift
                    tiles = [
                        jnp.where(keep, tiles[0], 0.0),
                        jnp.where(keep, tiles[1], tiles[0]),
                        jnp.where(keep, tiles[2], tiles[1]),
                        jnp.where(keep, 0.0, tiles[2]),
                    ]
                else:
                    tiles = tiles + [jnp.zeros((8, 128), jnp.float32)]
                parts = tiles if parts is None else [x + y for x, y in zip(parts, tiles)]
            parts = [part.astype(jnp.int32) for part in parts]
            total = parts if total is None else [x + y for x, y in zip(total, parts)]
        return total

    def finish(point):
        values = []
        for r4 in range(CHUNK_ROWS):
            totals = [shifted_sums(sum_scrs[point], r4, b) for b in range(3)]
            before = jnp.zeros((8, 128), jnp.float32)
            row = []
            for t in range(4):
                s0, s1, s2 = (total[t] for total in totals)
                quotient = (
                    s2.astype(jnp.float32) * (65536.0 / modulus)
                    + s1.astype(jnp.float32) * (256.0 / modulus)
                    + s0.astype(jnp.float32) * (1.0 / modulus)
                )
                quotient = ((quotient + ROUND) - ROUND).astype(jnp.int32)
                rest = (s2 << 16) + (s1 << 8) + s0 - quotient - ((quotient * 7) << 20)
                value = rest.astype(jnp.float32)
                shifted = pltpu.roll(value, 16, 1)
                row.append(value + sign * jnp.where(lane < 16, before, shifted))
                before = shifted
            values.append(row)
        for t in range(4):
            tiles = [row[t] for row in values]
            tiles = exchange_bit(tiles, 1, 1)
            tiles = exchange_bit(tiles, 1, 4)
            tiles = exchange_bit(tiles, 2, 2)
            for index, tile in enumerate(tiles):
                device = 4 * t + 2 * (index & 1) + (index >> 1)
                out_ref[pl.ds(device * 8 * PER + STEP * step + point, 8, stride=PER), :] = tile

    prepare(0)
    for point in range(STEP):
        if point + 1 < STEP:
            prepare(point + 1)
        multiply(point)
        if point:
            finish(point - 1)
    finish(STEP - 1)


def product(sign, left, right):
    return pl.pallas_call(
        product_kernel,
        grid=(PER // STEP,),
        in_specs=[pl.BlockSpec(memory_space=pltpu.SMEM)]
        + [pl.BlockSpec((POINTS, 128), lambda step, tile=tile: (0, tile)) for tile in range(2)]
        + [pl.BlockSpec((STEP, 256, 768), lambda step: (step, 0, 0))],
        out_specs=pl.BlockSpec((POINTS, 128), lambda step: (0, 0)),
        out_shape=jax.ShapeDtypeStruct((POINTS, 128), jnp.float32),
        scratch_shapes=[pltpu.VMEM((CHUNK_ROWS * 128, 256), jnp.bfloat16)] * STEP
        + [pltpu.VMEM((CHUNK_ROWS * 128, 768), jnp.float32)] * STEP,
        compiler_params=pltpu.CompilerParams(vmem_limit_bytes=VMEM_LIMIT),
        cost_estimate=pl.CostEstimate(
            flops=12 * 10**9, bytes_accessed=9 * 2**20, transcendentals=0
        ),
        name="product",
    )(sign, left, left, right)


def exchange(values):
    parts = values.reshape(N_DEV, PER, values.shape[1])
    moved = lax.all_to_all(parts, AXES, split_axis=0, concat_axis=0, tiled=True)
    return moved.reshape(values.shape)


def on_device(left, right):
    mine = lax.axis_index("deg") * N_ROW + lax.axis_index("row")
    sign = (1 - 2 * ((mine // 2) % 2)).astype(jnp.float32).reshape(1)
    first = exchange(forward((left, 0), (left, 1), (right, 0)))
    second = exchange(forward((left, 2), (left, 3)))
    factor = weights(first, 2)
    return backward([exchange(product(sign, part, factor)) for part in (first, second)])


def solution(mesh):
    return jax.shard_map(
        on_device,
        mesh=mesh,
        in_specs=(P("deg", "row"), P("deg", "row")),
        out_specs=P("deg", "row"),
        check_vma=False,
    )
```

```python
import functools

import jax
import jax.numpy as jnp
import numpy as np
from jax import lax
from jax.experimental import pallas as pl
from jax.experimental.pallas import tpu as pltpu
from jax.sharding import PartitionSpec as P

K = 64
COLS = 16
modulus = 7340033
generator = 3

BLOCK = 1024
POINTS = 2048
N_DEG = 16
N_ROW = 8
N_DEV = N_DEG * N_ROW
PER = POINTS // N_DEV
FACTORS = (64, 32)
AXES = ("deg", "row")
CHUNKS = 2
CHUNK_ROWS = 4
STEP = 2
PITCH = 40
PITCH_BACK = 72
UNROLL = 16

ROUND = 1.5 * 2.0**23
ROUND_8 = ROUND * 2.0**8
ROUND_16 = ROUND * 2.0**16
HIGH = 7.0 * 2.0**20


def root_powers(order):
    root = pow(generator, (modulus - 1) // order, modulus)
    values = np.ones(order, dtype=np.int64)
    for position in range(1, order):
        values[position] = values[position - 1] * root % modulus
    return values


def digit_matrix(matrix):
    columns = []
    for a in range(3):
        value = matrix * pow(2, 8 * a, modulus) % modulus
        value = np.where(value > modulus // 2, value - modulus, value)
        low = ((value + 128) & 255) - 128
        value = (value - low) >> 8
        middle = ((value + 128) & 255) - 128
        high = (value - middle) >> 8
        rows = np.concatenate([low, middle, high], axis=-2)
        columns.append(rows * 2.0 ** (-8 * a))
    return np.concatenate(columns, axis=-1).astype(np.float32)


def forward_tables():
    powers = root_powers(POINTS)
    k1, m1, m0 = np.arange(64), np.arange(32), np.arange(32)
    first = powers[(32 * m1[None, None, :] + m0[:, None, None]) * k1[None, :, None] % POINTS]
    k0 = np.arange(32)
    second = powers[64 * k0[:, None] * m0[None, :] % POINTS]
    return digit_matrix(first), digit_matrix(second)


def backward_tables():
    powers = root_powers(POINTS)
    k1, k0, m0, m1 = np.arange(64), np.arange(32), np.arange(32), np.arange(32)
    exponent = m0[None, :, None] * (64 * k0[None, None, :] + k1[:, None, None])
    first = powers[-exponent % POINTS] * pow(POINTS, modulus - 2, modulus) % modulus
    second = powers[-32 * m1[:, None] * k1[None, :] % POINTS]
    return digit_matrix(first), digit_matrix(second)


def split(value):
    high = (value + ROUND_16) - ROUND_16
    rest = value - high
    middle = (rest + ROUND_8) - ROUND_8
    return rest - middle, middle, high


def digit_rows(value):
    return jnp.concatenate([digit.astype(jnp.bfloat16) for digit in split(value)], axis=0)


def fold(sums):
    s0, s1, s2 = sums
    quotient = s2 * (65536.0 / modulus) + s1 * (256.0 / modulus)
    quotient = (quotient + ROUND) - ROUND
    return ((s2 * 65536.0 - quotient * HIGH) + s1 * 256.0) + (s0 - quotient)


def times_256(value):
    quotient = (value * (256.0 / modulus) + ROUND) - ROUND
    return (value * 256.0 - quotient * HIGH) - quotient


def matmul(first, second):
    return jnp.dot(first, second, preferred_element_type=jnp.float32)


def thirds(value):
    rows = value.shape[0] // 3
    return value[:rows], value[rows : 2 * rows], value[2 * rows :]


def in_parts(source, target, sems, first_sem, parts):
    rows = source.shape[0] // parts
    return [
        pltpu.make_async_copy(
            source.at[pl.ds(part * rows, rows)],
            target.at[pl.ds(part * rows, rows)],
            sems.at[first_sem + part],
        )
        for part in range(parts)
    ]


def forward_kernel(columns, first_hbm, second_hbm, *refs):
    tiles = len(columns)
    x_hbms, out_hbm, first_ref, second_ref, out_ref = refs[:tiles], *refs[tiles : tiles + 4]
    x_refs, middle_refs = refs[tiles + 4 : 2 * tiles + 4], refs[2 * tiles + 4 : 3 * tiles + 4]
    sems = refs[-1]
    x_copies = [
        pltpu.make_async_copy(
            x_hbm.at[:, :, pl.ds(tile * 128, 128)], x_ref.at[:, pl.ds(0, 32), :], sems.at[index]
        )
        for index, (x_hbm, x_ref, tile) in enumerate(zip(x_hbms, x_refs, columns))
    ]
    first_copies = in_parts(first_hbm, first_ref, sems, tiles, 2)
    second_copy = pltpu.make_async_copy(second_hbm, second_ref, sems.at[tiles + 2])
    out_copies = in_parts(out_ref, out_hbm, sems, tiles + 3, 4)
    for copy in x_copies + first_copies + [second_copy]:
        copy.start()
    for copy in x_copies:
        copy.wait()
    x_refs = [ref.reshape(32 * PITCH, 128) for ref in x_refs]

    def first_step(m0, carry):
        value = jnp.concatenate([ref[pl.ds(m0, 32, stride=PITCH), :] for ref in x_refs], axis=1)
        value = fold(thirds(matmul(first_ref[m0], digit_rows(value))))
        for tile, ref in enumerate(middle_refs):
            ref[pl.ds(m0, 64, stride=PITCH), :] = value[:, 128 * tile : 128 * tile + 128]
        return carry

    for part in range(2):
        first_copies[part].wait()
        lax.fori_loop(part * 16, part * 16 + 16, first_step, 0, unroll=UNROLL)
    second_copy.wait()
    second = second_ref[...]

    def second_step(k1, carry):
        rows = pl.ds(pl.multiple_of(k1 * PITCH, 8), 32)
        value = jnp.concatenate([ref[rows, :] for ref in middle_refs], axis=1)
        rows = pl.ds(pl.multiple_of(k1 * 32, 32), 32)
        out_ref[rows, :] = fold(thirds(matmul(second, digit_rows(value))))
        return carry

    for part in range(4):
        lax.fori_loop(part * 16, part * 16 + 16, second_step, 0, unroll=UNROLL)
        out_copies[part].start()
    for copy in out_copies:
        copy.wait()


ANYWHERE = pl.BlockSpec(memory_space=pl.ANY)


def forward(*columns):
    first, second = (jnp.asarray(table, dtype=jnp.bfloat16) for table in forward_tables())
    tiles = len(columns)
    return pl.pallas_call(
        functools.partial(forward_kernel, [tile for _, tile in columns]),
        in_specs=[ANYWHERE] * (2 + tiles),
        out_specs=ANYWHERE,
        out_shape=jax.ShapeDtypeStruct((POINTS, tiles * 128), jnp.float32),
        scratch_shapes=[
            pltpu.VMEM(first.shape, jnp.bfloat16),
            pltpu.VMEM(second.shape, jnp.bfloat16),
            pltpu.VMEM((POINTS, tiles * 128), jnp.float32),
        ]
        + [pltpu.VMEM((32, PITCH, 128), jnp.float32)] * tiles
        + [pltpu.VMEM((64 * PITCH, 128), jnp.float32)] * tiles
        + [pltpu.SemaphoreType.DMA((tiles + 7,))],
        compiler_params=pltpu.CompilerParams(vmem_limit_bytes=60 * 2**20),
        cost_estimate=pl.CostEstimate(
            flops=tiles * 3 * 10**9, bytes_accessed=tiles * 3 * 2**19, transcendentals=0
        ),
        name="forward",
    )(first, second, *[array.reshape(32, 32, -1) for array, _ in columns])


def backward_kernel(chunk, first_ref, second_ref, x_ref, *refs):
    before_ref = refs[0] if chunk else None
    out_ref, middle_ref = refs[-2:]
    low_half = lax.broadcasted_iota(jnp.int32, (32, 128), 1) < 64

    def first_step(k1, carry):
        rows = pl.ds(pl.multiple_of(k1 * 32, 32), 32)
        value = fold(thirds(matmul(first_ref[k1], digit_rows(x_ref[rows, :]))))
        middle_ref[pl.ds(k1, 32, stride=PITCH_BACK), :] = value
        return carry

    lax.fori_loop(0, 64, first_step, 0, unroll=UNROLL)
    second = second_ref[...]

    def second_step(m0, carry):
        rows = pl.ds(pl.multiple_of(m0 * PITCH_BACK, 8), 64)
        value = fold(thirds(matmul(second, digit_rows(middle_ref[rows, :]))))
        value = jnp.where(value < 0.0, value + float(modulus), value) / float(modulus)
        other = pltpu.roll(value, 64, 1)
        for e in range(2):
            place = pl.ds(e * BLOCK + m0, 32, stride=32)
            mine = value if e == chunk else other
            if chunk:
                mine = jnp.where(low_half, before_ref[place, :], mine)
            out_ref[place, :] = mine
        return carry

    lax.fori_loop(0, 32, second_step, 0, unroll=UNROLL)


def backward(values, chunk, before):
    first, second = (jnp.asarray(table, dtype=jnp.bfloat16) for table in backward_tables())
    return pl.pallas_call(
        functools.partial(backward_kernel, chunk),
        out_shape=jax.ShapeDtypeStruct((2 * BLOCK, 128), jnp.float32),
        scratch_shapes=[pltpu.VMEM((32 * PITCH_BACK, 128), jnp.float32)],
        compiler_params=pltpu.CompilerParams(vmem_limit_bytes=32 * 2**20),
        cost_estimate=pl.CostEstimate(
            flops=5 * 10**9, bytes_accessed=3 * 2**20, transcendentals=0
        ),
        name="backward",
    )(first, second, values, *before)


def exchange_bit(tiles, index_bit, group_bit):
    tiles = list(tiles)
    lane = lax.broadcasted_iota(jnp.int32, tiles[0].shape, 1)
    keep = (lane & (16 * group_bit)) == 0
    for low in range(len(tiles)):
        if low & index_bit:
            continue
        first, second = tiles[low], tiles[low + index_bit]
        tiles[low] = jnp.where(keep, first, pltpu.roll(second, 16 * group_bit, 1))
        tiles[low + index_bit] = jnp.where(
            keep, pltpu.roll(first, 128 - 16 * group_bit, 1), second
        )
    return tiles


def weights_kernel(right_ref, out_ref, *scratch):
    step = pl.program_id(0)
    for point in range(STEP):
        scrs = scratch[2 * point : 2 * point + 2]
        for half in range(2):
            tiles = [
                right_ref[pl.ds((half * 8 + d) * 8 * PER + STEP * step + point, 8, stride=PER), :]
                for d in range(8)
            ]
            for bit in (1, 2, 4):
                tiles = exchange_bit(tiles, bit, bit)
            for i8, tile in enumerate(tiles):
                scrs[half][pl.ds(i8, 8, stride=8), :] = tile
        value = jnp.concatenate([scr[...] for scr in scrs], axis=1)
        for a in range(3):
            if a:
                value = times_256(value)
            for b, digit in enumerate(split(value)):
                digit = (digit * 2.0 ** (-8 * (a + b))).astype(jnp.bfloat16)
                out_ref[point, a * 64 : a * 64 + 64, b * 256 : b * 256 + 256] = digit
                if a == 2:
                    out_ref[point, 192:256, b * 256 : b * 256 + 256] = digit


def weights(points, tile):
    return pl.pallas_call(
        weights_kernel,
        grid=(PER // STEP,),
        in_specs=[pl.BlockSpec((POINTS, 128), lambda step: (0, tile))],
        out_specs=pl.BlockSpec((STEP, 256, 768), lambda step: (step, 0, 0)),
        out_shape=jax.ShapeDtypeStruct((PER, 256, 768), jnp.bfloat16),
        scratch_shapes=[pltpu.VMEM((64, 128), jnp.float32)] * (2 * STEP),
        compiler_params=pltpu.CompilerParams(vmem_limit_bytes=32 * 2**20),
        cost_estimate=pl.CostEstimate(
            flops=3 * 10**9, bytes_accessed=7 * 2**20, transcendentals=0
        ),
        name="weights",
    )(points)


def product_kernel(sign_ref, *refs):
    left_refs, weight_ref, out_ref = refs[:2], refs[2], refs[3]
    left_scrs, sum_scrs = refs[4 : 4 + STEP], refs[4 + STEP :]
    step = pl.program_id(0)
    lane = lax.broadcasted_iota(jnp.int32, (8, 128), 1)
    low_half = lane < 64
    sign = sign_ref[0]

    def prepare(point):
        for pair in range(CHUNK_ROWS // 2):
            rows = [[], []]
            for d in range(N_DEG):
                tile = left_refs[pair][
                    pl.ds(d * 8 * PER + STEP * step + point, 8, stride=PER), :
                ]
                d0, d1, d2 = split(tile)
                d0_other, d1_other = pltpu.roll(d0, 64, 1), pltpu.roll(d1, 64, 1)
                rows[0].append(
                    (jnp.where(low_half, d0, d1_other), jnp.where(low_half, d2, 0.0))
                )
                rows[1].append(
                    (jnp.where(low_half, d0_other, d1), jnp.where(low_half, 0.0, d2))
                )
            for odd in range(2):
                start = (2 * pair + odd) * 128
                for part in range(2):
                    left_scrs[point][start : start + 128, part * 128 : part * 128 + 128] = (
                        jnp.concatenate([row[part] for row in rows[odd]], axis=0).astype(
                            jnp.bfloat16
                        )
                    )

    def multiply(point):
        sum_scrs[point][...] = matmul(left_scrs[point][...], weight_ref[point])

    def shifted_sums(sum_scr, r4, b):
        total = None
        for group in ((0, 1, 2), (3, 4, 5), (6, 7)):
            parts = None
            for shift in group:
                tiles = [
                    [
                        sum_scr[
                            pl.ds(r4 * 128 + (8 * high + shift) * 8, 8),
                            b * 256 + 128 * t : b * 256 + 128 * t + 128,
                        ]
                        for t in range(2)
                    ]
                    for high in range(2)
                ]
                tiles = [tiles[0][0], tiles[0][1] + tiles[1][0], tiles[1][1]]
                if shift:
                    tiles = [pltpu.roll(tile, 16 * shift, 1) for tile in tiles]
                    keep = lane >= 16 * shift
                    tiles = [
                        jnp.where(keep, tiles[0], 0.0),
                        jnp.where(keep, tiles[1], tiles[0]),
                        jnp.where(keep, tiles[2], tiles[1]),
                        jnp.where(keep, 0.0, tiles[2]),
                    ]
                else:
                    tiles = tiles + [jnp.zeros((8, 128), jnp.float32)]
                parts = tiles if parts is None else [x + y for x, y in zip(parts, tiles)]
            parts = [part.astype(jnp.int32) for part in parts]
            total = parts if total is None else [x + y for x, y in zip(total, parts)]
        return total

    def finish(point):
        values = []
        for r4 in range(CHUNK_ROWS):
            totals = [shifted_sums(sum_scrs[point], r4, b) for b in range(3)]
            before = jnp.zeros((8, 128), jnp.float32)
            row = []
            for t in range(4):
                s0, s1, s2 = (total[t] for total in totals)
                quotient = (
                    s2.astype(jnp.float32) * (65536.0 / modulus)
                    + s1.astype(jnp.float32) * (256.0 / modulus)
                    + s0.astype(jnp.float32) * (1.0 / modulus)
                )
                quotient = ((quotient + ROUND) - ROUND).astype(jnp.int32)
                rest = (s2 << 16) + (s1 << 8) + s0 - quotient - ((quotient * 7) << 20)
                value = rest.astype(jnp.float32)
                shifted = pltpu.roll(value, 16, 1)
                row.append(value + sign * jnp.where(lane < 16, before, shifted))
                before = shifted
            values.append(row)
        for t in range(4):
            tiles = [row[t] for row in values]
            tiles = exchange_bit(tiles, 1, 1)
            tiles = exchange_bit(tiles, 1, 4)
            tiles = exchange_bit(tiles, 2, 2)
            for index, tile in enumerate(tiles):
                device = 4 * t + 2 * (index & 1) + (index >> 1)
                out_ref[pl.ds(device * 8 * PER + STEP * step + point, 8, stride=PER), :] = tile

    prepare(0)
    for point in range(STEP):
        if point + 1 < STEP:
            prepare(point + 1)
        multiply(point)
        if point:
            finish(point - 1)
    finish(STEP - 1)


def product(sign, left, right):
    return pl.pallas_call(
        product_kernel,
        grid=(PER // STEP,),
        in_specs=[pl.BlockSpec(memory_space=pltpu.SMEM)]
        + [pl.BlockSpec((POINTS, 128), lambda step, tile=tile: (0, tile)) for tile in range(2)]
        + [pl.BlockSpec((STEP, 256, 768), lambda step: (step, 0, 0))],
        out_specs=pl.BlockSpec((POINTS, 128), lambda step: (0, 0)),
        out_shape=jax.ShapeDtypeStruct((POINTS, 128), jnp.float32),
        scratch_shapes=[pltpu.VMEM((CHUNK_ROWS * 128, 256), jnp.bfloat16)] * STEP
        + [pltpu.VMEM((CHUNK_ROWS * 128, 768), jnp.float32)] * STEP,
        compiler_params=pltpu.CompilerParams(vmem_limit_bytes=60 * 2**20),
        cost_estimate=pl.CostEstimate(
            flops=12 * 10**9, bytes_accessed=9 * 2**20, transcendentals=0
        ),
        name="product",
    )(sign, left, left, right)


def exchange(values):
    parts = values.reshape(N_DEV, PER, values.shape[1])
    moved = lax.all_to_all(parts, AXES, split_axis=0, concat_axis=0, tiled=True)
    return moved.reshape(values.shape)


def on_device(left, right):
    mine = lax.axis_index("deg") * N_ROW + lax.axis_index("row")
    sign = (1 - 2 * ((mine // 2) % 2)).astype(jnp.float32).reshape(1)
    first = exchange(forward((left, 0), (left, 1), (right, 0)))
    second = exchange(forward((left, 2), (left, 3)))
    factor = weights(first, 2)
    result = []
    for chunk, part in enumerate((first, second)):
        result = [backward(exchange(product(sign, part, factor)), chunk, result)]
    return result[0]


def solution(mesh):
    return jax.shard_map(
        on_device,
        mesh=mesh,
        in_specs=(P("deg", "row"), P("deg", "row")),
        out_specs=P("deg", "row"),
        check_vma=False,
    )
```

```python
import functools

import jax
import jax.numpy as jnp
import numpy as np
from jax import lax
from jax.experimental import pallas as pl
from jax.experimental.pallas import tpu as pltpu
from jax.sharding import PartitionSpec as P

K = 64
COLS = 16
modulus = 7340033
generator = 3

BLOCK = 1024
POINTS = 2048
N_DEG = 16
N_ROW = 8
N_DEV = N_DEG * N_ROW
PER = POINTS // N_DEV
FACTORS = (64, 32)
AXES = ("deg", "row")
CHUNKS = 2
CHUNK_ROWS = 4
STEP = 2
PITCH = 40
PITCH_BACK = 72
UNROLL = 16
BACK_LIMIT = 51

ROUND = 1.5 * 2.0**23
ROUND_8 = ROUND * 2.0**8
ROUND_16 = ROUND * 2.0**16
HIGH = 7.0 * 2.0**20


def root_powers(order):
    root = pow(generator, (modulus - 1) // order, modulus)
    values = np.ones(order, dtype=np.int64)
    for position in range(1, order):
        values[position] = values[position - 1] * root % modulus
    return values


def digit_matrix(matrix):
    columns = []
    for a in range(3):
        value = matrix * pow(2, 8 * a, modulus) % modulus
        value = np.where(value > modulus // 2, value - modulus, value)
        low = ((value + 128) & 255) - 128
        value = (value - low) >> 8
        middle = ((value + 128) & 255) - 128
        high = (value - middle) >> 8
        rows = np.concatenate([low, middle, high], axis=-2)
        columns.append(rows * 2.0 ** (-8 * a))
    return np.concatenate(columns, axis=-1).astype(np.float32)


def forward_tables():
    powers = root_powers(POINTS)
    k1, m1, m0 = np.arange(64), np.arange(32), np.arange(32)
    first = powers[(32 * m1[None, None, :] + m0[:, None, None]) * k1[None, :, None] % POINTS]
    k0 = np.arange(32)
    second = powers[64 * k0[:, None] * m0[None, :] % POINTS]
    return digit_matrix(first), digit_matrix(second)


def backward_tables():
    powers = root_powers(POINTS)
    k1, k0, m0, m1 = np.arange(64), np.arange(32), np.arange(32), np.arange(32)
    exponent = m0[None, :, None] * (64 * k0[None, None, :] + k1[:, None, None])
    first = powers[-exponent % POINTS] * pow(POINTS, modulus - 2, modulus) % modulus
    second = powers[-32 * m1[:, None] * k1[None, :] % POINTS]
    return digit_matrix(first), digit_matrix(second)


def split(value):
    high = (value + ROUND_16) - ROUND_16
    rest = value - high
    middle = (rest + ROUND_8) - ROUND_8
    return rest - middle, middle, high


def digit_rows(value):
    return jnp.concatenate([digit.astype(jnp.bfloat16) for digit in split(value)], axis=0)


def fold(sums):
    s0, s1, s2 = sums
    quotient = s2 * (65536.0 / modulus) + s1 * (256.0 / modulus)
    quotient = (quotient + ROUND) - ROUND
    return ((s2 * 65536.0 - quotient * HIGH) + s1 * 256.0) + (s0 - quotient)


def times_256(value):
    quotient = (value * (256.0 / modulus) + ROUND) - ROUND
    return (value * 256.0 - quotient * HIGH) - quotient


def matmul(first, second):
    return jnp.dot(first, second, preferred_element_type=jnp.float32)


def thirds(value):
    rows = value.shape[0] // 3
    return value[:rows], value[rows : 2 * rows], value[2 * rows :]


def in_parts(source, target, sems, first_sem, parts):
    rows = source.shape[0] // parts
    return [
        pltpu.make_async_copy(
            source.at[pl.ds(part * rows, rows)],
            target.at[pl.ds(part * rows, rows)],
            sems.at[first_sem + part],
        )
        for part in range(parts)
    ]


def forward_kernel(columns, first_hbm, second_hbm, *refs):
    tiles = len(columns)
    x_hbms, out_hbm, first_ref, second_ref, out_ref = refs[:tiles], *refs[tiles : tiles + 4]
    x_refs, middle_refs = refs[tiles + 4 : 2 * tiles + 4], refs[2 * tiles + 4 : 3 * tiles + 4]
    sems = refs[-1]
    x_copies = [
        pltpu.make_async_copy(
            x_hbm.at[:, :, pl.ds(tile * 128, 128)], x_ref.at[:, pl.ds(0, 32), :], sems.at[index]
        )
        for index, (x_hbm, x_ref, tile) in enumerate(zip(x_hbms, x_refs, columns))
    ]
    first_copies = in_parts(first_hbm, first_ref, sems, tiles, 2)
    second_copy = pltpu.make_async_copy(second_hbm, second_ref, sems.at[tiles + 2])
    out_copies = in_parts(out_ref, out_hbm, sems, tiles + 3, 4)
    for copy in x_copies + first_copies + [second_copy]:
        copy.start()
    for copy in x_copies:
        copy.wait()
    x_refs = [ref.reshape(32 * PITCH, 128) for ref in x_refs]

    def first_step(m0, carry):
        value = jnp.concatenate([ref[pl.ds(m0, 32, stride=PITCH), :] for ref in x_refs], axis=1)
        value = fold(thirds(matmul(first_ref[m0], digit_rows(value))))
        for tile, ref in enumerate(middle_refs):
            ref[pl.ds(m0, 64, stride=PITCH), :] = value[:, 128 * tile : 128 * tile + 128]
        return carry

    for part in range(2):
        first_copies[part].wait()
        lax.fori_loop(part * 16, part * 16 + 16, first_step, 0, unroll=UNROLL)
    second_copy.wait()
    second = second_ref[...]

    def second_step(k1, carry):
        rows = pl.ds(pl.multiple_of(k1 * PITCH, 8), 32)
        value = jnp.concatenate([ref[rows, :] for ref in middle_refs], axis=1)
        rows = pl.ds(pl.multiple_of(k1 * 32, 32), 32)
        out_ref[rows, :] = fold(thirds(matmul(second, digit_rows(value))))
        return carry

    for part in range(4):
        lax.fori_loop(part * 16, part * 16 + 16, second_step, 0, unroll=UNROLL)
        out_copies[part].start()
    for copy in out_copies:
        copy.wait()


ANYWHERE = pl.BlockSpec(memory_space=pl.ANY)


def forward(*columns):
    first, second = (jnp.asarray(table, dtype=jnp.bfloat16) for table in forward_tables())
    tiles = len(columns)
    return pl.pallas_call(
        functools.partial(forward_kernel, [tile for _, tile in columns]),
        in_specs=[ANYWHERE] * (2 + tiles),
        out_specs=ANYWHERE,
        out_shape=jax.ShapeDtypeStruct((POINTS, tiles * 128), jnp.float32),
        scratch_shapes=[
            pltpu.VMEM(first.shape, jnp.bfloat16),
            pltpu.VMEM(second.shape, jnp.bfloat16),
            pltpu.VMEM((POINTS, tiles * 128), jnp.float32),
        ]
        + [pltpu.VMEM((32, PITCH, 128), jnp.float32)] * tiles
        + [pltpu.VMEM((64 * PITCH, 128), jnp.float32)] * tiles
        + [pltpu.SemaphoreType.DMA((tiles + 7,))],
        compiler_params=pltpu.CompilerParams(vmem_limit_bytes=60 * 2**20),
        cost_estimate=pl.CostEstimate(
            flops=tiles * 3 * 10**9, bytes_accessed=tiles * 3 * 2**19, transcendentals=0
        ),
        name="forward",
    )(first, second, *[array.reshape(32, 32, -1) for array, _ in columns])


def backward_kernel(chunk, first_hbm, second_hbm, x_hbm, *refs):
    before_hbm, out_hbm = (refs[0], refs[1]) if chunk else (None, None)
    if chunk:
        first_ref, second_ref, x_ref, middle_ref, sems, before_ref, out_ref = refs[2:]
        out_copies = [
            [
                pltpu.make_async_copy(
                    out_ref.at[e, :, pl.ds(part * 16, 16), :],
                    out_hbm.at[e, :, pl.ds(part * 16, 16), :],
                    sems.at[10 + 2 * part + e],
                )
                for e in range(2)
            ]
            for part in range(2)
        ]
        padded_ref = out_ref.reshape(2 * 32 * PITCH, 128)
    else:
        out_ref, first_ref, second_ref, x_ref, middle_ref, sems = refs
    first_copies = in_parts(first_hbm, first_ref, sems, 0, 4)
    x_copies = in_parts(x_hbm, x_ref, sems, 4, 4)
    last_copies = [pltpu.make_async_copy(second_hbm, second_ref, sems.at[8])]
    if chunk:
        last_copies.append(pltpu.make_async_copy(before_hbm, before_ref, sems.at[9]))
    for pair in zip(x_copies, first_copies):
        for copy in pair:
            copy.start()
    for copy in last_copies:
        copy.start()
    low_half = lax.broadcasted_iota(jnp.int32, (32, 128), 1) < 64

    def first_step(k1, carry):
        rows = pl.ds(pl.multiple_of(k1 * 32, 32), 32)
        value = fold(thirds(matmul(first_ref[k1], digit_rows(x_ref[rows, :]))))
        middle_ref[pl.ds(k1, 32, stride=PITCH_BACK), :] = value
        return carry

    for part in range(4):
        x_copies[part].wait()
        first_copies[part].wait()
        lax.fori_loop(part * 16, part * 16 + 16, first_step, 0, unroll=UNROLL)
    for copy in last_copies:
        copy.wait()
    second = second_ref[...]

    def second_step(m0, carry):
        rows = pl.ds(pl.multiple_of(m0 * PITCH_BACK, 8), 64)
        value = fold(thirds(matmul(second, digit_rows(middle_ref[rows, :]))))
        value = jnp.where(value < 0.0, value + float(modulus), value) / float(modulus)
        other = pltpu.roll(value, 64, 1)
        for e in range(2):
            place = pl.ds(pl.multiple_of(e * BLOCK + m0 * 32, 32), 32)
            mine = value if e == chunk else other
            if chunk:
                mine = jnp.where(low_half, before_ref[place, :], mine)
                padded_ref[pl.ds(e * 32 * PITCH + m0, 32, stride=PITCH), :] = mine
            else:
                out_ref[place, :] = mine
        return carry

    for part in range(2):
        lax.fori_loop(part * 16, part * 16 + 16, second_step, 0, unroll=UNROLL)
        if chunk:
            for copy in out_copies[part]:
                copy.start()
    if chunk:
        for copy in out_copies[0] + out_copies[1]:
            copy.wait()


def backward(values, chunk, before):
    first, second = (jnp.asarray(table, dtype=jnp.bfloat16) for table in backward_tables())
    last = {"out_specs": ANYWHERE} if chunk else {}
    result = pl.pallas_call(
        functools.partial(backward_kernel, chunk),
        in_specs=[ANYWHERE] * (3 + chunk),
        out_shape=jax.ShapeDtypeStruct(
            (2, 32, 32, 128) if chunk else (2 * BLOCK, 128), jnp.float32
        ),
        scratch_shapes=[
            pltpu.VMEM(first.shape, jnp.bfloat16),
            pltpu.VMEM(second.shape, jnp.bfloat16),
            pltpu.VMEM((POINTS, 128), jnp.float32),
            pltpu.VMEM((32 * PITCH_BACK, 128), jnp.float32),
            pltpu.SemaphoreType.DMA((14,)),
        ]
        + [
            pltpu.VMEM((POINTS, 128), jnp.float32),
            pltpu.VMEM((2, 32, PITCH, 128), jnp.float32),
        ]
        * chunk,
        compiler_params=pltpu.CompilerParams(vmem_limit_bytes=BACK_LIMIT * 2**20),
        cost_estimate=pl.CostEstimate(
            flops=5 * 10**9, bytes_accessed=3 * 2**20, transcendentals=0
        ),
        name="backward",
        **last,
    )(first, second, values, *before)
    return result.reshape(2 * BLOCK, 128)


def exchange_bit(tiles, index_bit, group_bit):
    tiles = list(tiles)
    lane = lax.broadcasted_iota(jnp.int32, tiles[0].shape, 1)
    keep = (lane & (16 * group_bit)) == 0
    for low in range(len(tiles)):
        if low & index_bit:
            continue
        first, second = tiles[low], tiles[low + index_bit]
        tiles[low] = jnp.where(keep, first, pltpu.roll(second, 16 * group_bit, 1))
        tiles[low + index_bit] = jnp.where(
            keep, pltpu.roll(first, 128 - 16 * group_bit, 1), second
        )
    return tiles


def weights_kernel(right_ref, out_ref, *scratch):
    step = pl.program_id(0)
    for point in range(STEP):
        scrs = scratch[2 * point : 2 * point + 2]
        for half in range(2):
            tiles = [
                right_ref[pl.ds((half * 8 + d) * 8 * PER + STEP * step + point, 8, stride=PER), :]
                for d in range(8)
            ]
            for bit in (1, 2, 4):
                tiles = exchange_bit(tiles, bit, bit)
            for i8, tile in enumerate(tiles):
                scrs[half][pl.ds(i8, 8, stride=8), :] = tile
        value = jnp.concatenate([scr[...] for scr in scrs], axis=1)
        for a in range(3):
            if a:
                value = times_256(value)
            for b, digit in enumerate(split(value)):
                digit = (digit * 2.0 ** (-8 * (a + b))).astype(jnp.bfloat16)
                out_ref[point, a * 64 : a * 64 + 64, b * 256 : b * 256 + 256] = digit
                if a == 2:
                    out_ref[point, 192:256, b * 256 : b * 256 + 256] = digit


def weights(points, tile):
    return pl.pallas_call(
        weights_kernel,
        grid=(PER // STEP,),
        in_specs=[pl.BlockSpec((POINTS, 128), lambda step: (0, tile))],
        out_specs=pl.BlockSpec((STEP, 256, 768), lambda step: (step, 0, 0)),
        out_shape=jax.ShapeDtypeStruct((PER, 256, 768), jnp.bfloat16),
        scratch_shapes=[pltpu.VMEM((64, 128), jnp.float32)] * (2 * STEP),
        compiler_params=pltpu.CompilerParams(vmem_limit_bytes=32 * 2**20),
        cost_estimate=pl.CostEstimate(
            flops=3 * 10**9, bytes_accessed=7 * 2**20, transcendentals=0
        ),
        name="weights",
    )(points)


def product_kernel(sign_ref, *refs):
    left_refs, weight_ref, out_ref = refs[:2], refs[2], refs[3]
    left_scrs, sum_scrs = refs[4 : 4 + STEP], refs[4 + STEP :]
    step = pl.program_id(0)
    lane = lax.broadcasted_iota(jnp.int32, (8, 128), 1)
    low_half = lane < 64
    sign = sign_ref[0]

    def prepare(point):
        for pair in range(CHUNK_ROWS // 2):
            rows = [[], []]
            for d in range(N_DEG):
                tile = left_refs[pair][
                    pl.ds(d * 8 * PER + STEP * step + point, 8, stride=PER), :
                ]
                d0, d1, d2 = split(tile)
                d0_other, d1_other = pltpu.roll(d0, 64, 1), pltpu.roll(d1, 64, 1)
                rows[0].append(
                    (jnp.where(low_half, d0, d1_other), jnp.where(low_half, d2, 0.0))
                )
                rows[1].append(
                    (jnp.where(low_half, d0_other, d1), jnp.where(low_half, 0.0, d2))
                )
            for odd in range(2):
                start = (2 * pair + odd) * 128
                for part in range(2):
                    left_scrs[point][start : start + 128, part * 128 : part * 128 + 128] = (
                        jnp.concatenate([row[part] for row in rows[odd]], axis=0).astype(
                            jnp.bfloat16
                        )
                    )

    def multiply(point):
        sum_scrs[point][...] = matmul(left_scrs[point][...], weight_ref[point])

    def shifted_sums(sum_scr, r4, b):
        total = None
        for group in ((0, 1, 2), (3, 4, 5), (6, 7)):
            parts = None
            for shift in group:
                tiles = [
                    [
                        sum_scr[
                            pl.ds(r4 * 128 + (8 * high + shift) * 8, 8),
                            b * 256 + 128 * t : b * 256 + 128 * t + 128,
                        ]
                        for t in range(2)
                    ]
                    for high in range(2)
                ]
                tiles = [tiles[0][0], tiles[0][1] + tiles[1][0], tiles[1][1]]
                if shift:
                    tiles = [pltpu.roll(tile, 16 * shift, 1) for tile in tiles]
                    keep = lane >= 16 * shift
                    tiles = [
                        jnp.where(keep, tiles[0], 0.0),
                        jnp.where(keep, tiles[1], tiles[0]),
                        jnp.where(keep, tiles[2], tiles[1]),
                        jnp.where(keep, 0.0, tiles[2]),
                    ]
                else:
                    tiles = tiles + [jnp.zeros((8, 128), jnp.float32)]
                parts = tiles if parts is None else [x + y for x, y in zip(parts, tiles)]
            parts = [part.astype(jnp.int32) for part in parts]
            total = parts if total is None else [x + y for x, y in zip(total, parts)]
        return total

    def finish(point):
        values = []
        for r4 in range(CHUNK_ROWS):
            totals = [shifted_sums(sum_scrs[point], r4, b) for b in range(3)]
            before = jnp.zeros((8, 128), jnp.float32)
            row = []
            for t in range(4):
                s0, s1, s2 = (total[t] for total in totals)
                quotient = (
                    s2.astype(jnp.float32) * (65536.0 / modulus)
                    + s1.astype(jnp.float32) * (256.0 / modulus)
                    + s0.astype(jnp.float32) * (1.0 / modulus)
                )
                quotient = ((quotient + ROUND) - ROUND).astype(jnp.int32)
                rest = (s2 << 16) + (s1 << 8) + s0 - quotient - ((quotient * 7) << 20)
                value = rest.astype(jnp.float32)
                shifted = pltpu.roll(value, 16, 1)
                row.append(value + sign * jnp.where(lane < 16, before, shifted))
                before = shifted
            values.append(row)
        for t in range(4):
            tiles = [row[t] for row in values]
            tiles = exchange_bit(tiles, 1, 1)
            tiles = exchange_bit(tiles, 1, 4)
            tiles = exchange_bit(tiles, 2, 2)
            for index, tile in enumerate(tiles):
                device = 4 * t + 2 * (index & 1) + (index >> 1)
                out_ref[pl.ds(device * 8 * PER + STEP * step + point, 8, stride=PER), :] = tile

    prepare(0)
    for point in range(STEP):
        if point + 1 < STEP:
            prepare(point + 1)
        multiply(point)
        if point:
            finish(point - 1)
    finish(STEP - 1)


def product(sign, left, right):
    return pl.pallas_call(
        product_kernel,
        grid=(PER // STEP,),
        in_specs=[pl.BlockSpec(memory_space=pltpu.SMEM)]
        + [pl.BlockSpec((POINTS, 128), lambda step, tile=tile: (0, tile)) for tile in range(2)]
        + [pl.BlockSpec((STEP, 256, 768), lambda step: (step, 0, 0))],
        out_specs=pl.BlockSpec((POINTS, 128), lambda step: (0, 0)),
        out_shape=jax.ShapeDtypeStruct((POINTS, 128), jnp.float32),
        scratch_shapes=[pltpu.VMEM((CHUNK_ROWS * 128, 256), jnp.bfloat16)] * STEP
        + [pltpu.VMEM((CHUNK_ROWS * 128, 768), jnp.float32)] * STEP,
        compiler_params=pltpu.CompilerParams(vmem_limit_bytes=60 * 2**20),
        cost_estimate=pl.CostEstimate(
            flops=12 * 10**9, bytes_accessed=9 * 2**20, transcendentals=0
        ),
        name="product",
    )(sign, left, left, right)


def exchange(values):
    parts = values.reshape(N_DEV, PER, values.shape[1])
    moved = lax.all_to_all(parts, AXES, split_axis=0, concat_axis=0, tiled=True)
    return moved.reshape(values.shape)


def on_device(left, right):
    mine = lax.axis_index("deg") * N_ROW + lax.axis_index("row")
    sign = (1 - 2 * ((mine // 2) % 2)).astype(jnp.float32).reshape(1)
    first = exchange(forward((left, 0), (left, 1), (right, 0)))
    second = exchange(forward((left, 2), (left, 3)))
    factor = weights(first, 2)
    result = []
    for chunk, part in enumerate((first, second)):
        result = [backward(exchange(product(sign, part, factor)), chunk, result)]
    return result[0]


def solution(mesh):
    return jax.shard_map(
        on_device,
        mesh=mesh,
        in_specs=(P("deg", "row"), P("deg", "row")),
        out_specs=P("deg", "row"),
        check_vma=False,
    )
```

```python
import functools

import jax
import jax.numpy as jnp
import numpy as np
from jax import lax
from jax.experimental import pallas as pl
from jax.experimental.pallas import tpu as pltpu
from jax.sharding import PartitionSpec as P

K = 64
COLS = 16
modulus = 7340033
generator = 3

BLOCK = 1024
POINTS = 2048
N_DEG = 16
N_ROW = 8
N_DEV = N_DEG * N_ROW
PER = POINTS // N_DEV
FACTORS = (64, 32)
AXES = ("deg", "row")
CHUNKS = 2
CHUNK_ROWS = 4
STEP = 2
PITCH = 40
PITCH_BACK = 72
UNROLL = 16
BACK_LIMIT = 51

ROUND = 1.5 * 2.0**23
ROUND_8 = ROUND * 2.0**8
ROUND_16 = ROUND * 2.0**16
HIGH = 7.0 * 2.0**20


def root_powers(order):
    root = pow(generator, (modulus - 1) // order, modulus)
    values = np.ones(order, dtype=np.int64)
    for position in range(1, order):
        values[position] = values[position - 1] * root % modulus
    return values


def digit_matrix(matrix):
    columns = []
    for a in range(3):
        value = matrix * pow(2, 8 * a, modulus) % modulus
        value = np.where(value > modulus // 2, value - modulus, value)
        low = ((value + 128) & 255) - 128
        value = (value - low) >> 8
        middle = ((value + 128) & 255) - 128
        high = (value - middle) >> 8
        rows = np.concatenate([low, middle * 2.0**8, high * 2.0**16], axis=-2)
        columns.append(rows * 2.0 ** (-8 * a))
    return np.concatenate(columns, axis=-1).astype(np.float32)


def forward_tables():
    powers = root_powers(POINTS)
    k1, m1, m0 = np.arange(64), np.arange(32), np.arange(32)
    first = powers[(32 * m1[None, None, :] + m0[:, None, None]) * k1[None, :, None] % POINTS]
    k0 = np.arange(32)
    second = powers[64 * k0[:, None] * m0[None, :] % POINTS]
    return digit_matrix(first), digit_matrix(second)


def backward_tables():
    powers = root_powers(POINTS)
    k1, k0, m0, m1 = np.arange(64), np.arange(32), np.arange(32), np.arange(32)
    exponent = m0[None, :, None] * (64 * k0[None, None, :] + k1[:, None, None])
    first = powers[-exponent % POINTS] * pow(POINTS, modulus - 2, modulus) % modulus
    second = powers[-32 * m1[:, None] * k1[None, :] % POINTS]
    return digit_matrix(first), digit_matrix(second)


def split(value):
    high = (value + ROUND_16) - ROUND_16
    rest = value - high
    middle = (rest + ROUND_8) - ROUND_8
    return rest - middle, middle, high


def digit_rows(value):
    return jnp.concatenate([digit.astype(jnp.bfloat16) for digit in split(value)], axis=0)


def fold(sums):
    s0, s1, s2 = sums
    quotient = ((s2 + s1) * (1.0 / modulus) + ROUND) - ROUND
    return ((s2 - quotient * HIGH) + s1) + (s0 - quotient)


def times_256(value):
    quotient = (value * (256.0 / modulus) + ROUND) - ROUND
    return (value * 256.0 - quotient * HIGH) - quotient


def matmul(first, second):
    return jnp.dot(first, second, preferred_element_type=jnp.float32)


def thirds(value):
    rows = value.shape[0] // 3
    return value[:rows], value[rows : 2 * rows], value[2 * rows :]


def in_parts(source, target, sems, first_sem, parts):
    rows = source.shape[0] // parts
    return [
        pltpu.make_async_copy(
            source.at[pl.ds(part * rows, rows)],
            target.at[pl.ds(part * rows, rows)],
            sems.at[first_sem + part],
        )
        for part in range(parts)
    ]


def forward_kernel(columns, first_hbm, second_hbm, *refs):
    tiles = len(columns)
    x_hbms, out_hbm, first_ref, second_ref, out_ref = refs[:tiles], *refs[tiles : tiles + 4]
    x_refs, middle_refs = refs[tiles + 4 : 2 * tiles + 4], refs[2 * tiles + 4 : 3 * tiles + 4]
    sems = refs[-1]
    x_copies = [
        pltpu.make_async_copy(
            x_hbm.at[:, :, pl.ds(tile * 128, 128)], x_ref.at[:, pl.ds(0, 32), :], sems.at[index]
        )
        for index, (x_hbm, x_ref, tile) in enumerate(zip(x_hbms, x_refs, columns))
    ]
    first_copies = in_parts(first_hbm, first_ref, sems, tiles, 2)
    second_copy = pltpu.make_async_copy(second_hbm, second_ref, sems.at[tiles + 2])
    out_copies = in_parts(out_ref, out_hbm, sems, tiles + 3, 4)
    for copy in x_copies + first_copies + [second_copy]:
        copy.start()
    for copy in x_copies:
        copy.wait()
    x_refs = [ref.reshape(32 * PITCH, 128) for ref in x_refs]

    def first_step(m0, carry):
        value = jnp.concatenate([ref[pl.ds(m0, 32, stride=PITCH), :] for ref in x_refs], axis=1)
        value = fold(thirds(matmul(first_ref[m0], digit_rows(value))))
        for tile, ref in enumerate(middle_refs):
            ref[pl.ds(m0, 64, stride=PITCH), :] = value[:, 128 * tile : 128 * tile + 128]
        return carry

    for part in range(2):
        first_copies[part].wait()
        lax.fori_loop(part * 16, part * 16 + 16, first_step, 0, unroll=UNROLL)
    second_copy.wait()
    second = second_ref[...]

    def second_step(k1, carry):
        rows = pl.ds(pl.multiple_of(k1 * PITCH, 8), 32)
        value = jnp.concatenate([ref[rows, :] for ref in middle_refs], axis=1)
        rows = pl.ds(pl.multiple_of(k1 * 32, 32), 32)
        out_ref[rows, :] = fold(thirds(matmul(second, digit_rows(value))))
        return carry

    for part in range(4):
        lax.fori_loop(part * 16, part * 16 + 16, second_step, 0, unroll=UNROLL)
        out_copies[part].start()
    for copy in out_copies:
        copy.wait()


ANYWHERE = pl.BlockSpec(memory_space=pl.ANY)


def forward(*columns):
    first, second = (jnp.asarray(table, dtype=jnp.bfloat16) for table in forward_tables())
    tiles = len(columns)
    return pl.pallas_call(
        functools.partial(forward_kernel, [tile for _, tile in columns]),
        in_specs=[ANYWHERE] * (2 + tiles),
        out_specs=ANYWHERE,
        out_shape=jax.ShapeDtypeStruct((POINTS, tiles * 128), jnp.float32),
        scratch_shapes=[
            pltpu.VMEM(first.shape, jnp.bfloat16),
            pltpu.VMEM(second.shape, jnp.bfloat16),
            pltpu.VMEM((POINTS, tiles * 128), jnp.float32),
        ]
        + [pltpu.VMEM((32, PITCH, 128), jnp.float32)] * tiles
        + [pltpu.VMEM((64 * PITCH, 128), jnp.float32)] * tiles
        + [pltpu.SemaphoreType.DMA((tiles + 7,))],
        compiler_params=pltpu.CompilerParams(vmem_limit_bytes=60 * 2**20),
        cost_estimate=pl.CostEstimate(
            flops=tiles * 3 * 10**9, bytes_accessed=tiles * 3 * 2**19, transcendentals=0
        ),
        name="forward",
    )(first, second, *[array.reshape(32, 32, -1) for array, _ in columns])


def backward_kernel(chunk, first_hbm, second_hbm, x_hbm, *refs):
    before_hbm, out_hbm = (refs[0], refs[1]) if chunk else (None, None)
    if chunk:
        first_ref, second_ref, x_ref, middle_ref, sems, before_ref, out_ref = refs[2:]
        out_copies = [
            [
                pltpu.make_async_copy(
                    out_ref.at[e, :, pl.ds(part * 16, 16), :],
                    out_hbm.at[e, :, pl.ds(part * 16, 16), :],
                    sems.at[10 + 2 * part + e],
                )
                for e in range(2)
            ]
            for part in range(2)
        ]
        padded_ref = out_ref.reshape(2 * 32 * PITCH, 128)
    else:
        out_ref, first_ref, second_ref, x_ref, middle_ref, sems = refs
    first_copies = in_parts(first_hbm, first_ref, sems, 0, 4)
    x_copies = in_parts(x_hbm, x_ref, sems, 4, 4)
    last_copies = [pltpu.make_async_copy(second_hbm, second_ref, sems.at[8])]
    if chunk:
        last_copies.append(pltpu.make_async_copy(before_hbm, before_ref, sems.at[9]))
    for pair in zip(x_copies, first_copies):
        for copy in pair:
            copy.start()
    for copy in last_copies:
        copy.start()
    low_half = lax.broadcasted_iota(jnp.int32, (32, 128), 1) < 64

    def first_step(k1, carry):
        rows = pl.ds(pl.multiple_of(k1 * 32, 32), 32)
        value = fold(thirds(matmul(first_ref[k1], digit_rows(x_ref[rows, :]))))
        middle_ref[pl.ds(k1, 32, stride=PITCH_BACK), :] = value
        return carry

    for part in range(4):
        x_copies[part].wait()
        first_copies[part].wait()
        lax.fori_loop(part * 16, part * 16 + 16, first_step, 0, unroll=UNROLL)
    for copy in last_copies:
        copy.wait()
    second = second_ref[...]

    def second_step(m0, carry):
        rows = pl.ds(pl.multiple_of(m0 * PITCH_BACK, 8), 64)
        value = fold(thirds(matmul(second, digit_rows(middle_ref[rows, :]))))
        value = jnp.where(value < 0.0, value + float(modulus), value) / float(modulus)
        other = pltpu.roll(value, 64, 1)
        for e in range(2):
            place = pl.ds(pl.multiple_of(e * BLOCK + m0 * 32, 32), 32)
            mine = value if e == chunk else other
            if chunk:
                mine = jnp.where(low_half, before_ref[place, :], mine)
                padded_ref[pl.ds(e * 32 * PITCH + m0, 32, stride=PITCH), :] = mine
            else:
                out_ref[place, :] = mine
        return carry

    for part in range(2):
        lax.fori_loop(part * 16, part * 16 + 16, second_step, 0, unroll=UNROLL)
        if chunk:
            for copy in out_copies[part]:
                copy.start()
    if chunk:
        for copy in out_copies[0] + out_copies[1]:
            copy.wait()


def backward(values, chunk, before):
    first, second = (jnp.asarray(table, dtype=jnp.bfloat16) for table in backward_tables())
    last = {"out_specs": ANYWHERE} if chunk else {}
    result = pl.pallas_call(
        functools.partial(backward_kernel, chunk),
        in_specs=[ANYWHERE] * (3 + chunk),
        out_shape=jax.ShapeDtypeStruct(
            (2, 32, 32, 128) if chunk else (2 * BLOCK, 128), jnp.float32
        ),
        scratch_shapes=[
            pltpu.VMEM(first.shape, jnp.bfloat16),
            pltpu.VMEM(second.shape, jnp.bfloat16),
            pltpu.VMEM((POINTS, 128), jnp.float32),
            pltpu.VMEM((32 * PITCH_BACK, 128), jnp.float32),
            pltpu.SemaphoreType.DMA((14,)),
        ]
        + [
            pltpu.VMEM((POINTS, 128), jnp.float32),
            pltpu.VMEM((2, 32, PITCH, 128), jnp.float32),
        ]
        * chunk,
        compiler_params=pltpu.CompilerParams(vmem_limit_bytes=BACK_LIMIT * 2**20),
        cost_estimate=pl.CostEstimate(
            flops=5 * 10**9, bytes_accessed=3 * 2**20, transcendentals=0
        ),
        name="backward",
        **last,
    )(first, second, values, *before)
    return result.reshape(2 * BLOCK, 128)


def exchange_bit(tiles, index_bit, group_bit):
    tiles = list(tiles)
    lane = lax.broadcasted_iota(jnp.int32, tiles[0].shape, 1)
    keep = (lane & (16 * group_bit)) == 0
    for low in range(len(tiles)):
        if low & index_bit:
            continue
        first, second = tiles[low], tiles[low + index_bit]
        tiles[low] = jnp.where(keep, first, pltpu.roll(second, 16 * group_bit, 1))
        tiles[low + index_bit] = jnp.where(
            keep, pltpu.roll(first, 128 - 16 * group_bit, 1), second
        )
    return tiles


def weights_kernel(right_ref, out_ref, *scratch):
    step = pl.program_id(0)
    for point in range(STEP):
        scrs = scratch[2 * point : 2 * point + 2]
        for half in range(2):
            tiles = [
                right_ref[pl.ds((half * 8 + d) * 8 * PER + STEP * step + point, 8, stride=PER), :]
                for d in range(8)
            ]
            for bit in (1, 2, 4):
                tiles = exchange_bit(tiles, bit, bit)
            for i8, tile in enumerate(tiles):
                scrs[half][pl.ds(i8, 8, stride=8), :] = tile
        value = jnp.concatenate([scr[...] for scr in scrs], axis=1)
        for a in range(3):
            if a:
                value = times_256(value)
            for b, digit in enumerate(split(value)):
                digit = (digit * 2.0 ** (-8 * (a + b))).astype(jnp.bfloat16)
                out_ref[point, a * 64 : a * 64 + 64, b * 256 : b * 256 + 256] = digit
                if a == 2:
                    out_ref[point, 192:256, b * 256 : b * 256 + 256] = digit


def weights(points, tile):
    return pl.pallas_call(
        weights_kernel,
        grid=(PER // STEP,),
        in_specs=[pl.BlockSpec((POINTS, 128), lambda step: (0, tile))],
        out_specs=pl.BlockSpec((STEP, 256, 768), lambda step: (step, 0, 0)),
        out_shape=jax.ShapeDtypeStruct((PER, 256, 768), jnp.bfloat16),
        scratch_shapes=[pltpu.VMEM((64, 128), jnp.float32)] * (2 * STEP),
        compiler_params=pltpu.CompilerParams(vmem_limit_bytes=32 * 2**20),
        cost_estimate=pl.CostEstimate(
            flops=3 * 10**9, bytes_accessed=7 * 2**20, transcendentals=0
        ),
        name="weights",
    )(points)


def product_kernel(sign_ref, *refs):
    left_refs, weight_ref, out_ref = refs[:2], refs[2], refs[3]
    left_scrs, sum_scrs = refs[4 : 4 + STEP], refs[4 + STEP :]
    step = pl.program_id(0)
    lane = lax.broadcasted_iota(jnp.int32, (8, 128), 1)
    low_half = lane < 64
    sign = sign_ref[0]

    def prepare(point):
        for pair in range(CHUNK_ROWS // 2):
            rows = [[], []]
            for d in range(N_DEG):
                tile = left_refs[pair][
                    pl.ds(d * 8 * PER + STEP * step + point, 8, stride=PER), :
                ]
                d0, d1, d2 = split(tile)
                d0_other, d1_other = pltpu.roll(d0, 64, 1), pltpu.roll(d1, 64, 1)
                rows[0].append(
                    (jnp.where(low_half, d0, d1_other), jnp.where(low_half, d2, 0.0))
                )
                rows[1].append(
                    (jnp.where(low_half, d0_other, d1), jnp.where(low_half, 0.0, d2))
                )
            for odd in range(2):
                start = (2 * pair + odd) * 128
                for part in range(2):
                    left_scrs[point][start : start + 128, part * 128 : part * 128 + 128] = (
                        jnp.concatenate([row[part] for row in rows[odd]], axis=0).astype(
                            jnp.bfloat16
                        )
                    )

    def multiply(point):
        sum_scrs[point][...] = matmul(left_scrs[point][...], weight_ref[point])

    def shifted_sums(sum_scr, r4, b):
        total = None
        for group in ((0, 1, 2), (3, 4, 5), (6, 7)):
            parts = None
            for shift in group:
                tiles = [
                    [
                        sum_scr[
                            pl.ds(r4 * 128 + (8 * high + shift) * 8, 8),
                            b * 256 + 128 * t : b * 256 + 128 * t + 128,
                        ]
                        for t in range(2)
                    ]
                    for high in range(2)
                ]
                tiles = [tiles[0][0], tiles[0][1] + tiles[1][0], tiles[1][1]]
                if shift:
                    tiles = [pltpu.roll(tile, 16 * shift, 1) for tile in tiles]
                    keep = lane >= 16 * shift
                    tiles = [
                        jnp.where(keep, tiles[0], 0.0),
                        jnp.where(keep, tiles[1], tiles[0]),
                        jnp.where(keep, tiles[2], tiles[1]),
                        jnp.where(keep, 0.0, tiles[2]),
                    ]
                else:
                    tiles = tiles + [jnp.zeros((8, 128), jnp.float32)]
                parts = tiles if parts is None else [x + y for x, y in zip(parts, tiles)]
            parts = [part.astype(jnp.int32) for part in parts]
            total = parts if total is None else [x + y for x, y in zip(total, parts)]
        return total

    def finish(point):
        values = []
        for r4 in range(CHUNK_ROWS):
            totals = [shifted_sums(sum_scrs[point], r4, b) for b in range(3)]
            before = jnp.zeros((8, 128), jnp.float32)
            row = []
            for t in range(4):
                s0, s1, s2 = (total[t] for total in totals)
                quotient = (
                    s2.astype(jnp.float32) * (65536.0 / modulus)
                    + s1.astype(jnp.float32) * (256.0 / modulus)
                    + s0.astype(jnp.float32) * (1.0 / modulus)
                )
                quotient = ((quotient + ROUND) - ROUND).astype(jnp.int32)
                rest = (s2 << 16) + (s1 << 8) + s0 - quotient - ((quotient * 7) << 20)
                value = rest.astype(jnp.float32)
                shifted = pltpu.roll(value, 16, 1)
                row.append(value + sign * jnp.where(lane < 16, before, shifted))
                before = shifted
            values.append(row)
        for t in range(4):
            tiles = [row[t] for row in values]
            tiles = exchange_bit(tiles, 1, 1)
            tiles = exchange_bit(tiles, 1, 4)
            tiles = exchange_bit(tiles, 2, 2)
            for index, tile in enumerate(tiles):
                device = 4 * t + 2 * (index & 1) + (index >> 1)
                out_ref[pl.ds(device * 8 * PER + STEP * step + point, 8, stride=PER), :] = tile

    prepare(0)
    for point in range(STEP):
        if point + 1 < STEP:
            prepare(point + 1)
        multiply(point)
        if point:
            finish(point - 1)
    finish(STEP - 1)


def product(sign, left, right):
    return pl.pallas_call(
        product_kernel,
        grid=(PER // STEP,),
        in_specs=[pl.BlockSpec(memory_space=pltpu.SMEM)]
        + [pl.BlockSpec((POINTS, 128), lambda step, tile=tile: (0, tile)) for tile in range(2)]
        + [pl.BlockSpec((STEP, 256, 768), lambda step: (step, 0, 0))],
        out_specs=pl.BlockSpec((POINTS, 128), lambda step: (0, 0)),
        out_shape=jax.ShapeDtypeStruct((POINTS, 128), jnp.float32),
        scratch_shapes=[pltpu.VMEM((CHUNK_ROWS * 128, 256), jnp.bfloat16)] * STEP
        + [pltpu.VMEM((CHUNK_ROWS * 128, 768), jnp.float32)] * STEP,
        compiler_params=pltpu.CompilerParams(vmem_limit_bytes=60 * 2**20),
        cost_estimate=pl.CostEstimate(
            flops=12 * 10**9, bytes_accessed=9 * 2**20, transcendentals=0
        ),
        name="product",
    )(sign, left, left, right)


def exchange(values):
    parts = values.reshape(N_DEV, PER, values.shape[1])
    moved = lax.all_to_all(parts, AXES, split_axis=0, concat_axis=0, tiled=True)
    return moved.reshape(values.shape)


def on_device(left, right):
    mine = lax.axis_index("deg") * N_ROW + lax.axis_index("row")
    sign = (1 - 2 * ((mine // 2) % 2)).astype(jnp.float32).reshape(1)
    first = exchange(forward((left, 0), (left, 1), (right, 0)))
    second = exchange(forward((left, 2), (left, 3)))
    factor = weights(first, 2)
    result = []
    for chunk, part in enumerate((first, second)):
        result = [backward(exchange(product(sign, part, factor)), chunk, result)]
    return result[0]


def solution(mesh):
    return jax.shard_map(
        on_device,
        mesh=mesh,
        in_specs=(P("deg", "row"), P("deg", "row")),
        out_specs=P("deg", "row"),
        check_vma=False,
    )
```

```python
import functools

import jax
import jax.numpy as jnp
import numpy as np
from jax import lax
from jax.experimental import pallas as pl
from jax.experimental.pallas import tpu as pltpu
from jax.sharding import PartitionSpec as P

K = 64
COLS = 16
modulus = 7340033
generator = 3

BLOCK = 1024
POINTS = 2048
N_DEG = 16
N_ROW = 8
N_DEV = N_DEG * N_ROW
PER = POINTS // N_DEV
FACTORS = (64, 32)
AXES = ("deg", "row")
CHUNKS = 2
CHUNK_ROWS = 4
STEP = 2
PITCH = 40
PITCH_BACK = 72
UNROLL = 16
BACK_LIMIT = 51

ROUND = 1.5 * 2.0**23
ROUND_8 = ROUND * 2.0**8
ROUND_16 = ROUND * 2.0**16
HIGH = 7.0 * 2.0**20


def root_powers(order):
    root = pow(generator, (modulus - 1) // order, modulus)
    values = np.ones(order, dtype=np.int64)
    for position in range(1, order):
        values[position] = values[position - 1] * root % modulus
    return values


def digit_matrix(matrix):
    columns = []
    for a in range(3):
        value = matrix * pow(2, 8 * a, modulus) % modulus
        value = np.where(value > modulus // 2, value - modulus, value)
        low = ((value + 128) & 255) - 128
        value = (value - low) >> 8
        middle = ((value + 128) & 255) - 128
        high = (value - middle) >> 8
        rows = np.concatenate([low, middle * 2.0**8, high * 2.0**16], axis=-2)
        columns.append(rows * 2.0 ** (-8 * a))
    return np.concatenate(columns, axis=-1).astype(np.float32)


def forward_tables():
    powers = root_powers(POINTS)
    k1, m1, m0 = np.arange(64), np.arange(32), np.arange(32)
    first = powers[(32 * m1[None, None, :] + m0[:, None, None]) * k1[None, :, None] % POINTS]
    k0 = np.arange(32)
    second = powers[64 * k0[:, None] * m0[None, :] % POINTS]
    return digit_matrix(first), digit_matrix(second)


def backward_tables():
    powers = root_powers(POINTS)
    k1, k0, m0, m1 = np.arange(64), np.arange(32), np.arange(32), np.arange(32)
    exponent = m0[None, :, None] * (64 * k0[None, None, :] + k1[:, None, None])
    first = powers[-exponent % POINTS] * pow(POINTS, modulus - 2, modulus) % modulus
    second = powers[-32 * m1[:, None] * k1[None, :] % POINTS]
    return digit_matrix(first), digit_matrix(second)


def split(value):
    high = (value + ROUND_16) - ROUND_16
    rest = value - high
    middle = (rest + ROUND_8) - ROUND_8
    return rest - middle, middle, high


def digit_rows(value):
    return jnp.concatenate([digit.astype(jnp.bfloat16) for digit in split(value)], axis=0)


def fold(sums):
    s0, s1, s2 = sums
    quotient = ((s2 + s1) * (1.0 / modulus) + ROUND) - ROUND
    return ((s2 - quotient * HIGH) + s1) + (s0 - quotient)


def times_256(value):
    quotient = (value * (256.0 / modulus) + ROUND) - ROUND
    return (value * 256.0 - quotient * HIGH) - quotient


def matmul(first, second):
    return jnp.dot(first, second, preferred_element_type=jnp.float32)


def thirds(value):
    rows = value.shape[0] // 3
    return value[:rows], value[rows : 2 * rows], value[2 * rows :]


def in_parts(source, target, sems, first_sem, parts):
    rows = source.shape[0] // parts
    return [
        pltpu.make_async_copy(
            source.at[pl.ds(part * rows, rows)],
            target.at[pl.ds(part * rows, rows)],
            sems.at[first_sem + part],
        )
        for part in range(parts)
    ]


def forward_kernel(columns, first_hbm, second_hbm, *refs):
    tiles = len(columns)
    x_hbms, out_hbm, first_ref, second_ref, out_ref = refs[:tiles], *refs[tiles : tiles + 4]
    x_refs, middle_refs = refs[tiles + 4 : 2 * tiles + 4], refs[2 * tiles + 4 : 3 * tiles + 4]
    sems = refs[-1]
    x_copies = [
        pltpu.make_async_copy(
            x_hbm.at[:, :, pl.ds(tile * 128, 128)], x_ref.at[:, pl.ds(0, 32), :], sems.at[index]
        )
        for index, (x_hbm, x_ref, tile) in enumerate(zip(x_hbms, x_refs, columns))
    ]
    first_copies = in_parts(first_hbm, first_ref, sems, tiles, 4)
    second_copy = pltpu.make_async_copy(second_hbm, second_ref, sems.at[tiles + 4])
    out_copies = in_parts(out_ref, out_hbm, sems, tiles + 5, 8)
    for copy in first_copies[:1] + x_copies + first_copies[1:] + [second_copy]:
        copy.start()
    for copy in x_copies:
        copy.wait()
    x_refs = [ref.reshape(32 * PITCH, 128) for ref in x_refs]

    def first_step(m0, carry):
        value = jnp.concatenate([ref[pl.ds(m0, 32, stride=PITCH), :] for ref in x_refs], axis=1)
        value = fold(thirds(matmul(first_ref[m0], digit_rows(value))))
        for tile, ref in enumerate(middle_refs):
            ref[pl.ds(m0, 64, stride=PITCH), :] = value[:, 128 * tile : 128 * tile + 128]
        return carry

    for part in range(4):
        first_copies[part].wait()
        lax.fori_loop(part * 8, part * 8 + 8, first_step, 0, unroll=8)
    second_copy.wait()
    second = second_ref[...]

    def second_step(k1, carry):
        rows = pl.ds(pl.multiple_of(k1 * PITCH, 8), 32)
        value = jnp.concatenate([ref[rows, :] for ref in middle_refs], axis=1)
        rows = pl.ds(pl.multiple_of(k1 * 32, 32), 32)
        out_ref[rows, :] = fold(thirds(matmul(second, digit_rows(value))))
        return carry

    for part in range(8):
        lax.fori_loop(part * 8, part * 8 + 8, second_step, 0, unroll=8)
        out_copies[part].start()
    for copy in out_copies:
        copy.wait()


ANYWHERE = pl.BlockSpec(memory_space=pl.ANY)


def forward(*columns):
    first, second = (jnp.asarray(table, dtype=jnp.bfloat16) for table in forward_tables())
    tiles = len(columns)
    return pl.pallas_call(
        functools.partial(forward_kernel, [tile for _, tile in columns]),
        in_specs=[ANYWHERE] * (2 + tiles),
        out_specs=ANYWHERE,
        out_shape=jax.ShapeDtypeStruct((POINTS, tiles * 128), jnp.float32),
        scratch_shapes=[
            pltpu.VMEM(first.shape, jnp.bfloat16),
            pltpu.VMEM(second.shape, jnp.bfloat16),
            pltpu.VMEM((POINTS, tiles * 128), jnp.float32),
        ]
        + [pltpu.VMEM((32, PITCH, 128), jnp.float32)] * tiles
        + [pltpu.VMEM((64 * PITCH, 128), jnp.float32)] * tiles
        + [pltpu.SemaphoreType.DMA((tiles + 13,))],
        compiler_params=pltpu.CompilerParams(vmem_limit_bytes=60 * 2**20),
        cost_estimate=pl.CostEstimate(
            flops=tiles * 3 * 10**9, bytes_accessed=tiles * 3 * 2**19, transcendentals=0
        ),
        name="forward",
    )(first, second, *[array.reshape(32, 32, -1) for array, _ in columns])


def backward_kernel(chunk, first_hbm, second_hbm, x_hbm, *refs):
    before_hbm, out_hbm = (refs[0], refs[1]) if chunk else (None, None)
    if chunk:
        first_ref, second_ref, x_ref, middle_ref, sems, before_ref, out_ref = refs[2:]
        out_copies = [
            [
                pltpu.make_async_copy(
                    out_ref.at[e, :, pl.ds(part * 16, 16), :],
                    out_hbm.at[e, :, pl.ds(part * 16, 16), :],
                    sems.at[10 + 2 * part + e],
                )
                for e in range(2)
            ]
            for part in range(2)
        ]
        padded_ref = out_ref.reshape(2 * 32 * PITCH, 128)
    else:
        out_ref, first_ref, second_ref, x_ref, middle_ref, sems = refs
    first_copies = in_parts(first_hbm, first_ref, sems, 0, 4)
    x_copies = in_parts(x_hbm, x_ref, sems, 4, 4)
    last_copies = [pltpu.make_async_copy(second_hbm, second_ref, sems.at[8])]
    if chunk:
        last_copies.append(pltpu.make_async_copy(before_hbm, before_ref, sems.at[9]))
    for pair in zip(x_copies, first_copies):
        for copy in pair:
            copy.start()
    for copy in last_copies:
        copy.start()
    low_half = lax.broadcasted_iota(jnp.int32, (32, 128), 1) < 64

    def first_step(k1, carry):
        rows = pl.ds(pl.multiple_of(k1 * 32, 32), 32)
        value = fold(thirds(matmul(first_ref[k1], digit_rows(x_ref[rows, :]))))
        middle_ref[pl.ds(k1, 32, stride=PITCH_BACK), :] = value
        return carry

    for part in range(4):
        x_copies[part].wait()
        first_copies[part].wait()
        lax.fori_loop(part * 16, part * 16 + 16, first_step, 0, unroll=UNROLL)
    for copy in last_copies:
        copy.wait()
    second = second_ref[...]

    def second_step(m0, carry):
        rows = pl.ds(pl.multiple_of(m0 * PITCH_BACK, 8), 64)
        value = fold(thirds(matmul(second, digit_rows(middle_ref[rows, :]))))
        value = jnp.where(value < 0.0, value + float(modulus), value) * (1.0 / modulus)
        other = pltpu.roll(value, 64, 1)
        for e in range(2):
            place = pl.ds(pl.multiple_of(e * BLOCK + m0 * 32, 32), 32)
            mine = value if e == chunk else other
            if chunk:
                mine = jnp.where(low_half, before_ref[place, :], mine)
                padded_ref[pl.ds(e * 32 * PITCH + m0, 32, stride=PITCH), :] = mine
            else:
                out_ref[place, :] = mine
        return carry

    for part in range(2):
        lax.fori_loop(part * 16, part * 16 + 16, second_step, 0, unroll=UNROLL)
        if chunk:
            for copy in out_copies[part]:
                copy.start()
    if chunk:
        for copy in out_copies[0] + out_copies[1]:
            copy.wait()


def backward(values, chunk, before):
    first, second = (jnp.asarray(table, dtype=jnp.bfloat16) for table in backward_tables())
    last = {"out_specs": ANYWHERE} if chunk else {}
    result = pl.pallas_call(
        functools.partial(backward_kernel, chunk),
        in_specs=[ANYWHERE] * (3 + chunk),
        out_shape=jax.ShapeDtypeStruct(
            (2, 32, 32, 128) if chunk else (2 * BLOCK, 128), jnp.float32
        ),
        scratch_shapes=[
            pltpu.VMEM(first.shape, jnp.bfloat16),
            pltpu.VMEM(second.shape, jnp.bfloat16),
            pltpu.VMEM((POINTS, 128), jnp.float32),
            pltpu.VMEM((32 * PITCH_BACK, 128), jnp.float32),
            pltpu.SemaphoreType.DMA((14,)),
        ]
        + [
            pltpu.VMEM((POINTS, 128), jnp.float32),
            pltpu.VMEM((2, 32, PITCH, 128), jnp.float32),
        ]
        * chunk,
        compiler_params=pltpu.CompilerParams(vmem_limit_bytes=BACK_LIMIT * 2**20),
        cost_estimate=pl.CostEstimate(
            flops=5 * 10**9, bytes_accessed=3 * 2**20, transcendentals=0
        ),
        name="backward",
        **last,
    )(first, second, values, *before)
    return result.reshape(2 * BLOCK, 128)


def exchange_bit(tiles, index_bit, group_bit):
    tiles = list(tiles)
    lane = lax.broadcasted_iota(jnp.int32, tiles[0].shape, 1)
    keep = (lane & (16 * group_bit)) == 0
    for low in range(len(tiles)):
        if low & index_bit:
            continue
        first, second = tiles[low], tiles[low + index_bit]
        tiles[low] = jnp.where(keep, first, pltpu.roll(second, 16 * group_bit, 1))
        tiles[low + index_bit] = jnp.where(
            keep, pltpu.roll(first, 128 - 16 * group_bit, 1), second
        )
    return tiles


def weights_kernel(right_ref, out_ref, *scratch):
    step = pl.program_id(0)
    for point in range(STEP):
        scrs = scratch[2 * point : 2 * point + 2]
        for half in range(2):
            tiles = [
                right_ref[pl.ds((half * 8 + d) * 8 * PER + STEP * step + point, 8, stride=PER), :]
                for d in range(8)
            ]
            for bit in (1, 2, 4):
                tiles = exchange_bit(tiles, bit, bit)
            for i8, tile in enumerate(tiles):
                scrs[half][pl.ds(i8, 8, stride=8), :] = tile
        value = jnp.concatenate([scr[...] for scr in scrs], axis=1)
        for a in range(3):
            if a:
                value = times_256(value)
            for b, digit in enumerate(split(value)):
                digit = (digit * 2.0 ** (-8 * (a + b))).astype(jnp.bfloat16)
                out_ref[point, a * 64 : a * 64 + 64, b * 256 : b * 256 + 256] = digit
                if a == 2:
                    out_ref[point, 192:256, b * 256 : b * 256 + 256] = digit


def weights(points, tile):
    return pl.pallas_call(
        weights_kernel,
        grid=(PER // STEP,),
        in_specs=[pl.BlockSpec((POINTS, 128), lambda step: (0, tile))],
        out_specs=pl.BlockSpec((STEP, 256, 768), lambda step: (step, 0, 0)),
        out_shape=jax.ShapeDtypeStruct((PER, 256, 768), jnp.bfloat16),
        scratch_shapes=[pltpu.VMEM((64, 128), jnp.float32)] * (2 * STEP),
        compiler_params=pltpu.CompilerParams(vmem_limit_bytes=32 * 2**20),
        cost_estimate=pl.CostEstimate(
            flops=3 * 10**9, bytes_accessed=7 * 2**20, transcendentals=0
        ),
        name="weights",
    )(points)


def product_kernel(sign_ref, *refs):
    left_refs, weight_ref, out_ref = refs[:2], refs[2], refs[3]
    left_scrs, sum_scrs = refs[4 : 4 + STEP], refs[4 + STEP :]
    step = pl.program_id(0)
    lane = lax.broadcasted_iota(jnp.int32, (8, 128), 1)
    low_half = lane < 64
    sign = sign_ref[0]

    def prepare(point):
        for pair in range(CHUNK_ROWS // 2):
            rows = [[], []]
            for d in range(N_DEG):
                tile = left_refs[pair][
                    pl.ds(d * 8 * PER + STEP * step + point, 8, stride=PER), :
                ]
                d0, d1, d2 = split(tile)
                d0_other, d1_other = pltpu.roll(d0, 64, 1), pltpu.roll(d1, 64, 1)
                rows[0].append(
                    (jnp.where(low_half, d0, d1_other), jnp.where(low_half, d2, 0.0))
                )
                rows[1].append(
                    (jnp.where(low_half, d0_other, d1), jnp.where(low_half, 0.0, d2))
                )
            for odd in range(2):
                start = (2 * pair + odd) * 128
                for part in range(2):
                    left_scrs[point][start : start + 128, part * 128 : part * 128 + 128] = (
                        jnp.concatenate([row[part] for row in rows[odd]], axis=0).astype(
                            jnp.bfloat16
                        )
                    )

    def multiply(point):
        sum_scrs[point][...] = matmul(left_scrs[point][...], weight_ref[point])

    def shifted_sums(sum_scr, r4, b):
        total = None
        for group in ((0, 1, 2), (3, 4, 5), (6, 7)):
            parts = None
            for shift in group:
                tiles = [
                    [
                        sum_scr[
                            pl.ds(r4 * 128 + (8 * high + shift) * 8, 8),
                            b * 256 + 128 * t : b * 256 + 128 * t + 128,
                        ]
                        for t in range(2)
                    ]
                    for high in range(2)
                ]
                tiles = [tiles[0][0], tiles[0][1] + tiles[1][0], tiles[1][1]]
                if shift:
                    tiles = [pltpu.roll(tile, 16 * shift, 1) for tile in tiles]
                    keep = lane >= 16 * shift
                    tiles = [
                        jnp.where(keep, tiles[0], 0.0),
                        jnp.where(keep, tiles[1], tiles[0]),
                        jnp.where(keep, tiles[2], tiles[1]),
                        jnp.where(keep, 0.0, tiles[2]),
                    ]
                else:
                    tiles = tiles + [jnp.zeros((8, 128), jnp.float32)]
                parts = tiles if parts is None else [x + y for x, y in zip(parts, tiles)]
            parts = [part.astype(jnp.int32) for part in parts]
            total = parts if total is None else [x + y for x, y in zip(total, parts)]
        return total

    def finish(point):
        values = []
        for r4 in range(CHUNK_ROWS):
            totals = [shifted_sums(sum_scrs[point], r4, b) for b in range(3)]
            before = jnp.zeros((8, 128), jnp.float32)
            row = []
            for t in range(4):
                s0, s1, s2 = (total[t] for total in totals)
                quotient = (
                    s2.astype(jnp.float32) * (65536.0 / modulus)
                    + s1.astype(jnp.float32) * (256.0 / modulus)
                    + s0.astype(jnp.float32) * (1.0 / modulus)
                )
                quotient = ((quotient + ROUND) - ROUND).astype(jnp.int32)
                rest = (s2 << 16) + (s1 << 8) + s0 - quotient - ((quotient * 7) << 20)
                value = rest.astype(jnp.float32)
                shifted = pltpu.roll(value, 16, 1)
                row.append(value + sign * jnp.where(lane < 16, before, shifted))
                before = shifted
            values.append(row)
        for t in range(4):
            tiles = [row[t] for row in values]
            tiles = exchange_bit(tiles, 1, 1)
            tiles = exchange_bit(tiles, 1, 4)
            tiles = exchange_bit(tiles, 2, 2)
            for index, tile in enumerate(tiles):
                device = 4 * t + 2 * (index & 1) + (index >> 1)
                out_ref[pl.ds(device * 8 * PER + STEP * step + point, 8, stride=PER), :] = tile

    prepare(0)
    for point in range(STEP):
        if point + 1 < STEP:
            prepare(point + 1)
        multiply(point)
        if point:
            finish(point - 1)
    finish(STEP - 1)


def product(sign, left, right):
    return pl.pallas_call(
        product_kernel,
        grid=(PER // STEP,),
        in_specs=[pl.BlockSpec(memory_space=pltpu.SMEM)]
        + [pl.BlockSpec((POINTS, 128), lambda step, tile=tile: (0, tile)) for tile in range(2)]
        + [pl.BlockSpec((STEP, 256, 768), lambda step: (step, 0, 0))],
        out_specs=pl.BlockSpec((POINTS, 128), lambda step: (0, 0)),
        out_shape=jax.ShapeDtypeStruct((POINTS, 128), jnp.float32),
        scratch_shapes=[pltpu.VMEM((CHUNK_ROWS * 128, 256), jnp.bfloat16)] * STEP
        + [pltpu.VMEM((CHUNK_ROWS * 128, 768), jnp.float32)] * STEP,
        compiler_params=pltpu.CompilerParams(vmem_limit_bytes=60 * 2**20),
        cost_estimate=pl.CostEstimate(
            flops=12 * 10**9, bytes_accessed=9 * 2**20, transcendentals=0
        ),
        name="product",
    )(sign, left, left, right)


def exchange(values):
    parts = values.reshape(N_DEV, PER, values.shape[1])
    moved = lax.all_to_all(parts, AXES, split_axis=0, concat_axis=0, tiled=True)
    return moved.reshape(values.shape)


def on_device(left, right):
    mine = lax.axis_index("deg") * N_ROW + lax.axis_index("row")
    sign = (1 - 2 * ((mine // 2) % 2)).astype(jnp.float32).reshape(1)
    first = exchange(forward((left, 0), (left, 1), (right, 0)))
    second = exchange(forward((left, 2), (left, 3)))
    factor = weights(first, 2)
    result = []
    for chunk, part in enumerate((first, second)):
        result = [backward(exchange(product(sign, part, factor)), chunk, result)]
    return result[0]


def solution(mesh):
    return jax.shard_map(
        on_device,
        mesh=mesh,
        in_specs=(P("deg", "row"), P("deg", "row")),
        out_specs=P("deg", "row"),
        check_vma=False,
    )
```

```python
import functools

import jax
import jax.numpy as jnp
import numpy as np
from jax import lax
from jax.experimental import pallas as pl
from jax.experimental.pallas import tpu as pltpu
from jax.sharding import PartitionSpec as P

K = 64
COLS = 16
modulus = 7340033
generator = 3

BLOCK = 1024
POINTS = 2048
N_DEG = 16
N_ROW = 8
N_DEV = N_DEG * N_ROW
PER = POINTS // N_DEV
FACTORS = (64, 32)
AXES = ("deg", "row")
CHUNKS = 2
CHUNK_ROWS = 4
STEP = 2
PITCH = 40
PITCH_BACK = 72
UNROLL = 16
BACK_LIMIT = 51

ROUND = 1.5 * 2.0**23
ROUND_8 = ROUND * 2.0**8
ROUND_16 = ROUND * 2.0**16
HIGH = 7.0 * 2.0**20


def root_powers(order):
    root = pow(generator, (modulus - 1) // order, modulus)
    values = np.ones(order, dtype=np.int64)
    for position in range(1, order):
        values[position] = values[position - 1] * root % modulus
    return values


def digit_matrix(matrix):
    columns = []
    for a in range(3):
        value = matrix * pow(2, 8 * a, modulus) % modulus
        value = np.where(value > modulus // 2, value - modulus, value)
        low = ((value + 128) & 255) - 128
        value = (value - low) >> 8
        middle = ((value + 128) & 255) - 128
        high = (value - middle) >> 8
        rows = np.concatenate([low, middle * 2.0**8, high * 2.0**16], axis=-2)
        columns.append(rows * 2.0 ** (-8 * a))
    return np.concatenate(columns, axis=-1).astype(np.float32)


def forward_tables():
    powers = root_powers(POINTS)
    k1, m1, m0 = np.arange(64), np.arange(32), np.arange(32)
    first = powers[(32 * m1[None, None, :] + m0[:, None, None]) * k1[None, :, None] % POINTS]
    k0 = np.arange(32)
    second = powers[64 * k0[:, None] * m0[None, :] % POINTS]
    return digit_matrix(first), digit_matrix(second)


def backward_tables():
    powers = root_powers(POINTS)
    k1, k0, m0, m1 = np.arange(64), np.arange(32), np.arange(32), np.arange(32)
    exponent = m0[None, :, None] * (64 * k0[None, None, :] + k1[:, None, None])
    first = powers[-exponent % POINTS] * pow(POINTS, modulus - 2, modulus) % modulus
    second = powers[-32 * m1[:, None] * k1[None, :] % POINTS]
    return digit_matrix(first), digit_matrix(second)


def split(value):
    high = (value + ROUND_16) - ROUND_16
    rest = value - high
    middle = (rest + ROUND_8) - ROUND_8
    return rest - middle, middle, high


def digit_rows(value):
    return jnp.concatenate([digit.astype(jnp.bfloat16) for digit in split(value)], axis=0)


def fold(sums):
    s0, s1, s2 = sums
    quotient = ((s2 + s1) * (1.0 / modulus) + ROUND) - ROUND
    return ((s2 - quotient * HIGH) + s1) + (s0 - quotient)


def times_256(value):
    quotient = (value * (256.0 / modulus) + ROUND) - ROUND
    return (value * 256.0 - quotient * HIGH) - quotient


def matmul(first, second):
    return jnp.dot(first, second, preferred_element_type=jnp.float32)


def thirds(value):
    rows = value.shape[0] // 3
    return value[:rows], value[rows : 2 * rows], value[2 * rows :]


def in_parts(source, target, sems, first_sem, parts):
    rows = source.shape[0] // parts
    return [
        pltpu.make_async_copy(
            source.at[pl.ds(part * rows, rows)],
            target.at[pl.ds(part * rows, rows)],
            sems.at[first_sem + part],
        )
        for part in range(parts)
    ]


def forward_kernel(columns, first_hbm, second_hbm, *refs):
    tiles = len(columns)
    x_hbms, out_hbm, first_ref, second_ref, out_ref = refs[:tiles], *refs[tiles : tiles + 4]
    x_refs, middle_refs = refs[tiles + 4 : 2 * tiles + 4], refs[2 * tiles + 4 : 3 * tiles + 4]
    sems = refs[-1]
    x_copies = [
        pltpu.make_async_copy(
            x_hbm.at[:, :, pl.ds(tile * 128, 128)], x_ref.at[:, pl.ds(0, 32), :], sems.at[index]
        )
        for index, (x_hbm, x_ref, tile) in enumerate(zip(x_hbms, x_refs, columns))
    ]
    first_copies = in_parts(first_hbm, first_ref, sems, tiles, 4)
    second_copy = pltpu.make_async_copy(second_hbm, second_ref, sems.at[tiles + 4])
    out_copies = in_parts(out_ref, out_hbm, sems, tiles + 5, 8)
    for copy in first_copies[:1] + x_copies + first_copies[1:] + [second_copy]:
        copy.start()
    for copy in x_copies:
        copy.wait()
    x_refs = [ref.reshape(32 * PITCH, 128) for ref in x_refs]

    def first_step(m0, carry):
        value = jnp.concatenate([ref[pl.ds(m0, 32, stride=PITCH), :] for ref in x_refs], axis=1)
        value = fold(thirds(matmul(first_ref[m0], digit_rows(value))))
        for tile, ref in enumerate(middle_refs):
            ref[pl.ds(m0, 64, stride=PITCH), :] = value[:, 128 * tile : 128 * tile + 128]
        return carry

    for part in range(4):
        first_copies[part].wait()
        lax.fori_loop(part * 8, part * 8 + 8, first_step, 0, unroll=8)
    second_copy.wait()
    second = second_ref[...]

    def second_step(k1, carry):
        rows = pl.ds(pl.multiple_of(k1 * PITCH, 8), 32)
        value = jnp.concatenate([ref[rows, :] for ref in middle_refs], axis=1)
        rows = pl.ds(pl.multiple_of(k1 * 32, 32), 32)
        out_ref[rows, :] = fold(thirds(matmul(second, digit_rows(value))))
        return carry

    for part in range(8):
        lax.fori_loop(part * 8, part * 8 + 8, second_step, 0, unroll=8)
        out_copies[part].start()
    for copy in out_copies:
        copy.wait()


ANYWHERE = pl.BlockSpec(memory_space=pl.ANY)


def forward(*columns):
    first, second = (jnp.asarray(table, dtype=jnp.bfloat16) for table in forward_tables())
    tiles = len(columns)
    return pl.pallas_call(
        functools.partial(forward_kernel, [tile for _, tile in columns]),
        in_specs=[ANYWHERE] * (2 + tiles),
        out_specs=ANYWHERE,
        out_shape=jax.ShapeDtypeStruct((POINTS, tiles * 128), jnp.float32),
        scratch_shapes=[
            pltpu.VMEM(first.shape, jnp.bfloat16),
            pltpu.VMEM(second.shape, jnp.bfloat16),
            pltpu.VMEM((POINTS, tiles * 128), jnp.float32),
        ]
        + [pltpu.VMEM((32, PITCH, 128), jnp.float32)] * tiles
        + [pltpu.VMEM((64 * PITCH, 128), jnp.float32)] * tiles
        + [pltpu.SemaphoreType.DMA((tiles + 13,))],
        compiler_params=pltpu.CompilerParams(vmem_limit_bytes=60 * 2**20),
        cost_estimate=pl.CostEstimate(
            flops=tiles * 3 * 10**9, bytes_accessed=tiles * 3 * 2**19, transcendentals=0
        ),
        name="forward",
    )(first, second, *[array.reshape(32, 32, -1) for array, _ in columns])


def backward_kernel(chunk, first_hbm, second_hbm, x_hbm, *refs):
    before_hbm, out_hbm = (refs[0], refs[1]) if chunk else (None, None)
    if chunk:
        first_ref, second_ref, x_ref, middle_ref, sems, before_ref, out_ref = refs[2:]
        out_copies = [
            [
                pltpu.make_async_copy(
                    out_ref.at[e, :, pl.ds(part * 8, 8), :],
                    out_hbm.at[e, :, pl.ds(part * 8, 8), :],
                    sems.at[10 + 2 * part + e],
                )
                for e in range(2)
            ]
            for part in range(4)
        ]
        padded_ref = out_ref.reshape(2 * 32 * PITCH, 128)
    else:
        out_ref, first_ref, second_ref, x_ref, middle_ref, sems = refs
    first_copies = in_parts(first_hbm, first_ref, sems, 0, 4)
    x_copies = in_parts(x_hbm, x_ref, sems, 4, 4)
    last_copies = [pltpu.make_async_copy(second_hbm, second_ref, sems.at[8])]
    if chunk:
        last_copies.append(pltpu.make_async_copy(before_hbm, before_ref, sems.at[9]))
    for pair in zip(x_copies, first_copies):
        for copy in pair:
            copy.start()
    for copy in last_copies:
        copy.start()
    low_half = lax.broadcasted_iota(jnp.int32, (32, 128), 1) < 64

    def first_step(k1, carry):
        rows = pl.ds(pl.multiple_of(k1 * 32, 32), 32)
        value = fold(thirds(matmul(first_ref[k1], digit_rows(x_ref[rows, :]))))
        middle_ref[pl.ds(k1, 32, stride=PITCH_BACK), :] = value
        return carry

    for part in range(4):
        x_copies[part].wait()
        first_copies[part].wait()
        lax.fori_loop(part * 16, part * 16 + 16, first_step, 0, unroll=UNROLL)
    for copy in last_copies:
        copy.wait()
    second = second_ref[...]

    def second_step(m0, carry):
        rows = pl.ds(pl.multiple_of(m0 * PITCH_BACK, 8), 64)
        value = fold(thirds(matmul(second, digit_rows(middle_ref[rows, :]))))
        value = jnp.where(value < 0.0, value + float(modulus), value) * (1.0 / modulus)
        other = pltpu.roll(value, 64, 1)
        for e in range(2):
            place = pl.ds(pl.multiple_of(e * BLOCK + m0 * 32, 32), 32)
            mine = value if e == chunk else other
            if chunk:
                mine = jnp.where(low_half, before_ref[place, :], mine)
                padded_ref[pl.ds(e * 32 * PITCH + m0, 32, stride=PITCH), :] = mine
            else:
                out_ref[place, :] = mine
        return carry

    for part in range(4):
        lax.fori_loop(part * 8, part * 8 + 8, second_step, 0, unroll=8)
        if chunk:
            for copy in out_copies[part]:
                copy.start()
    if chunk:
        for copy in sum(out_copies, []):
            copy.wait()


def backward(values, chunk, before):
    first, second = (jnp.asarray(table, dtype=jnp.bfloat16) for table in backward_tables())
    last = {"out_specs": ANYWHERE} if chunk else {}
    result = pl.pallas_call(
        functools.partial(backward_kernel, chunk),
        in_specs=[ANYWHERE] * (3 + chunk),
        out_shape=jax.ShapeDtypeStruct(
            (2, 32, 32, 128) if chunk else (2 * BLOCK, 128), jnp.float32
        ),
        scratch_shapes=[
            pltpu.VMEM(first.shape, jnp.bfloat16),
            pltpu.VMEM(second.shape, jnp.bfloat16),
            pltpu.VMEM((POINTS, 128), jnp.float32),
            pltpu.VMEM((32 * PITCH_BACK, 128), jnp.float32),
            pltpu.SemaphoreType.DMA((18,)),
        ]
        + [
            pltpu.VMEM((POINTS, 128), jnp.float32),
            pltpu.VMEM((2, 32, PITCH, 128), jnp.float32),
        ]
        * chunk,
        compiler_params=pltpu.CompilerParams(vmem_limit_bytes=BACK_LIMIT * 2**20),
        cost_estimate=pl.CostEstimate(
            flops=5 * 10**9, bytes_accessed=3 * 2**20, transcendentals=0
        ),
        name="backward",
        **last,
    )(first, second, values, *before)
    return result.reshape(2 * BLOCK, 128)


def exchange_bit(tiles, index_bit, group_bit):
    tiles = list(tiles)
    lane = lax.broadcasted_iota(jnp.int32, tiles[0].shape, 1)
    keep = (lane & (16 * group_bit)) == 0
    for low in range(len(tiles)):
        if low & index_bit:
            continue
        first, second = tiles[low], tiles[low + index_bit]
        tiles[low] = jnp.where(keep, first, pltpu.roll(second, 16 * group_bit, 1))
        tiles[low + index_bit] = jnp.where(
            keep, pltpu.roll(first, 128 - 16 * group_bit, 1), second
        )
    return tiles


def weights_kernel(right_ref, out_ref, *scratch):
    step = pl.program_id(0)
    for point in range(STEP):
        scrs = scratch[2 * point : 2 * point + 2]
        for half in range(2):
            tiles = [
                right_ref[pl.ds((half * 8 + d) * 8 * PER + STEP * step + point, 8, stride=PER), :]
                for d in range(8)
            ]
            for bit in (1, 2, 4):
                tiles = exchange_bit(tiles, bit, bit)
            for i8, tile in enumerate(tiles):
                scrs[half][pl.ds(i8, 8, stride=8), :] = tile
        value = jnp.concatenate([scr[...] for scr in scrs], axis=1)
        for a in range(3):
            if a:
                value = times_256(value)
            for b, digit in enumerate(split(value)):
                digit = (digit * 2.0 ** (-8 * (a + b))).astype(jnp.bfloat16)
                out_ref[point, a * 64 : a * 64 + 64, b * 256 : b * 256 + 256] = digit
                if a == 2:
                    out_ref[point, 192:256, b * 256 : b * 256 + 256] = digit


def weights(points, tile):
    return pl.pallas_call(
        weights_kernel,
        grid=(PER // STEP,),
        in_specs=[pl.BlockSpec((POINTS, 128), lambda step: (0, tile))],
        out_specs=pl.BlockSpec((STEP, 256, 768), lambda step: (step, 0, 0)),
        out_shape=jax.ShapeDtypeStruct((PER, 256, 768), jnp.bfloat16),
        scratch_shapes=[pltpu.VMEM((64, 128), jnp.float32)] * (2 * STEP),
        compiler_params=pltpu.CompilerParams(vmem_limit_bytes=32 * 2**20),
        cost_estimate=pl.CostEstimate(
            flops=3 * 10**9, bytes_accessed=7 * 2**20, transcendentals=0
        ),
        name="weights",
    )(points)


def product_kernel(sign_ref, *refs):
    left_refs, weight_ref, out_ref = refs[:2], refs[2], refs[3]
    left_scrs, sum_scrs = refs[4 : 4 + STEP], refs[4 + STEP :]
    step = pl.program_id(0)
    lane = lax.broadcasted_iota(jnp.int32, (8, 128), 1)
    low_half = lane < 64
    sign = sign_ref[0]

    def prepare(point):
        for pair in range(CHUNK_ROWS // 2):
            rows = [[], []]
            for d in range(N_DEG):
                tile = left_refs[pair][
                    pl.ds(d * 8 * PER + STEP * step + point, 8, stride=PER), :
                ]
                d0, d1, d2 = split(tile)
                d0_other, d1_other = pltpu.roll(d0, 64, 1), pltpu.roll(d1, 64, 1)
                rows[0].append(
                    (jnp.where(low_half, d0, d1_other), jnp.where(low_half, d2, 0.0))
                )
                rows[1].append(
                    (jnp.where(low_half, d0_other, d1), jnp.where(low_half, 0.0, d2))
                )
            for odd in range(2):
                start = (2 * pair + odd) * 128
                for part in range(2):
                    left_scrs[point][start : start + 128, part * 128 : part * 128 + 128] = (
                        jnp.concatenate([row[part] for row in rows[odd]], axis=0).astype(
                            jnp.bfloat16
                        )
                    )

    def multiply(point):
        sum_scrs[point][...] = matmul(left_scrs[point][...], weight_ref[point])

    def shifted_sums(sum_scr, r4, b):
        total = None
        for group in ((0, 1, 2), (3, 4, 5), (6, 7)):
            parts = None
            for shift in group:
                tiles = [
                    [
                        sum_scr[
                            pl.ds(r4 * 128 + (8 * high + shift) * 8, 8),
                            b * 256 + 128 * t : b * 256 + 128 * t + 128,
                        ]
                        for t in range(2)
                    ]
                    for high in range(2)
                ]
                tiles = [tiles[0][0], tiles[0][1] + tiles[1][0], tiles[1][1]]
                if shift:
                    tiles = [pltpu.roll(tile, 16 * shift, 1) for tile in tiles]
                    keep = lane >= 16 * shift
                    tiles = [
                        jnp.where(keep, tiles[0], 0.0),
                        jnp.where(keep, tiles[1], tiles[0]),
                        jnp.where(keep, tiles[2], tiles[1]),
                        jnp.where(keep, 0.0, tiles[2]),
                    ]
                else:
                    tiles = tiles + [jnp.zeros((8, 128), jnp.float32)]
                parts = tiles if parts is None else [x + y for x, y in zip(parts, tiles)]
            parts = [part.astype(jnp.int32) for part in parts]
            total = parts if total is None else [x + y for x, y in zip(total, parts)]
        return total

    def finish(point):
        values = []
        for r4 in range(CHUNK_ROWS):
            totals = [shifted_sums(sum_scrs[point], r4, b) for b in range(3)]
            before = jnp.zeros((8, 128), jnp.float32)
            row = []
            for t in range(4):
                s0, s1, s2 = (total[t] for total in totals)
                quotient = (
                    s2.astype(jnp.float32) * (65536.0 / modulus)
                    + s1.astype(jnp.float32) * (256.0 / modulus)
                    + s0.astype(jnp.float32) * (1.0 / modulus)
                )
                quotient = ((quotient + ROUND) - ROUND).astype(jnp.int32)
                rest = (s2 << 16) + (s1 << 8) + s0 - quotient - ((quotient * 7) << 20)
                value = rest.astype(jnp.float32)
                shifted = pltpu.roll(value, 16, 1)
                row.append(value + sign * jnp.where(lane < 16, before, shifted))
                before = shifted
            values.append(row)
        for t in range(4):
            tiles = [row[t] for row in values]
            tiles = exchange_bit(tiles, 1, 1)
            tiles = exchange_bit(tiles, 1, 4)
            tiles = exchange_bit(tiles, 2, 2)
            for index, tile in enumerate(tiles):
                device = 4 * t + 2 * (index & 1) + (index >> 1)
                out_ref[pl.ds(device * 8 * PER + STEP * step + point, 8, stride=PER), :] = tile

    prepare(0)
    for point in range(STEP):
        if point + 1 < STEP:
            prepare(point + 1)
        multiply(point)
        if point:
            finish(point - 1)
    finish(STEP - 1)


def product(sign, left, right):
    return pl.pallas_call(
        product_kernel,
        grid=(PER // STEP,),
        in_specs=[pl.BlockSpec(memory_space=pltpu.SMEM)]
        + [pl.BlockSpec((POINTS, 128), lambda step, tile=tile: (0, tile)) for tile in range(2)]
        + [pl.BlockSpec((STEP, 256, 768), lambda step: (step, 0, 0))],
        out_specs=pl.BlockSpec((POINTS, 128), lambda step: (0, 0)),
        out_shape=jax.ShapeDtypeStruct((POINTS, 128), jnp.float32),
        scratch_shapes=[pltpu.VMEM((CHUNK_ROWS * 128, 256), jnp.bfloat16)] * STEP
        + [pltpu.VMEM((CHUNK_ROWS * 128, 768), jnp.float32)] * STEP,
        compiler_params=pltpu.CompilerParams(vmem_limit_bytes=60 * 2**20),
        cost_estimate=pl.CostEstimate(
            flops=12 * 10**9, bytes_accessed=9 * 2**20, transcendentals=0
        ),
        name="product",
    )(sign, left, left, right)


def exchange(values):
    parts = values.reshape(N_DEV, PER, values.shape[1])
    moved = lax.all_to_all(parts, AXES, split_axis=0, concat_axis=0, tiled=True)
    return moved.reshape(values.shape)


def on_device(left, right):
    mine = lax.axis_index("deg") * N_ROW + lax.axis_index("row")
    sign = (1 - 2 * ((mine // 2) % 2)).astype(jnp.float32).reshape(1)
    first = exchange(forward((left, 0), (left, 1), (right, 0)))
    second = exchange(forward((left, 2), (left, 3)))
    factor = weights(first, 2)
    result = []
    for chunk, part in enumerate((first, second)):
        result = [backward(exchange(product(sign, part, factor)), chunk, result)]
    return result[0]


def solution(mesh):
    return jax.shard_map(
        on_device,
        mesh=mesh,
        in_specs=(P("deg", "row"), P("deg", "row")),
        out_specs=P("deg", "row"),
        check_vma=False,
    )
```
